32 devices in a mesh: groups: 2 (over y), dp: 8 (over z, x), tensor: 2 (over core).
Axes of the slice: x: 2, y: 2, z: 4, core: 2. Of those that a mesh axis runs over, the one named last changes fastest.
Arguments:
- layer_input: bfloat16 [8192, 4096], P(('groups', 'dp'), 'tensor'), parts along dimension 0, may hold values from -6 to 6
- gate_grad: bfloat16 [8192, 14336], P(('groups', 'dp'), 'tensor'), parts along dimension 0, may hold values from -6 to 6
- factor_in: bfloat16 [64, 4096], P(None, 'tensor'), may hold values from -0.09375 to 0.09375
- factor_out: bfloat16 [64, 14336], P(None, 'tensor'), may hold values from -0.046875 to 0.046875
- precondition: float32 [4096, 4096], P(('dp', 'tensor')), may hold values from -0.09375 to 0.09375
- query_grads: bfloat16 [1024, 4096], P(('dp', 'tensor')), may hold values from -6 to 6
Outputs:
- influence: float32 [16, 1024], P('groups', ('dp', 'tensor')), parts along dimension 0
The draws below stay inside these ranges and needn't reach their ends.
There are 2 independent parts, one for each index of `groups`. The reference program is written for one: setup_inputs(seed, part) draws one part's arguments, and reference() takes and returns one part's arrays. A program takes and returns all parts, laid end to end along the dimension named above; an argument that names none is the same for every part. Nothing has to cross between parts.
All inputs are finite; a program needn't handle non-finite values.
Results may differ from the reference program's by a relative error of at most 0.0029.
Values may be sent and summed in bfloat16 or wider, within the bound.
No kernel may reach another device: no remote copies, remote signals or barrier semaphores. Data moves between devices by JAX's collectives and lax.ppermute only.
A program may use at most 64 MiB of HBM per device.

```python
import math
import jax
import jax.numpy as jnp
from jax import lax

D = 4096
FF = 14336
KP = 64
TOK_SEQ = 512
SEQS = 8
KK = 4096
TOKENS = 4096
NQ = 1024


def block_scale(stream_key, shape, shards, least, high):
    gain, own = 1.0, jax.random.fold_in(stream_key, 6)
    for axis_at, shards_of in shards:
        heights = jnp.exp(jax.random.uniform(jax.random.fold_in(own, axis_at), (shards_of,), jnp.float32, least / len(shards), high / len(shards)))
        gain = gain * jnp.repeat(heights, shape[axis_at] // shards_of).reshape([-1 if axis == axis_at else 1 for axis in range(len(shape))])
    return gain


def normal_values(stream_key, extent, deviation, most, pieces=(), dtype=jnp.bfloat16):
    drawn = jax.random.normal(stream_key, extent, jnp.float32) * deviation
    if len(pieces) > 0:
        drawn = block_scale(stream_key, extent, pieces, -0.22, 0.18) * drawn
    return jnp.clip(drawn, min=-most, max=most).astype(dtype)


def setup_inputs(seed: int = 0, part: int = 0) -> dict:
    key_of = jax.random.split(jax.random.key(seed), 7)
    part_splits = jax.random.split(jax.random.fold_in(key_of[6], part), 7)
    layer_input = normal_values(part_splits[0], (TOKENS, D), 1.0, 6.0, ((0, 8), (1, 2)))
    gate_grad = normal_values(part_splits[1], (TOKENS, FF), 1.0, 6.0, ((0, 8), (1, 2)))
    factor_in = normal_values(key_of[2], (KP, D), D ** -0.5, 0.09375, ((1, 2),))
    factor_out = normal_values(key_of[3], (KP, FF), FF ** -0.5, 0.046875, ((1, 2),))
    precondition = normal_values(key_of[4], (KK, KK), KK ** -0.5, 0.09375, ((0, 16),), jnp.float32)
    query_grads = normal_values(key_of[5], (NQ, KK), 1.0, 6.0, ((0, 16),))
    return {"layer_input": layer_input, "gate_grad": gate_grad, "factor_in": factor_in, "factor_out": factor_out, "precondition": precondition, "query_grads": query_grads}


def reference(layer_input, gate_grad, factor_in, factor_out, precondition, query_grads):
    inner_side = jnp.dot(layer_input, factor_in.T, preferred_element_type=jnp.float32)
    outer_side = jnp.dot(gate_grad, factor_out.T, preferred_element_type=jnp.float32)
    sequence_grads = jnp.einsum('sta,stb->sab', inner_side.reshape(SEQS, TOK_SEQ, KP), outer_side.reshape(SEQS, TOK_SEQ, KP), precision=lax.Precision.HIGHEST)
    sequence_grads = sequence_grads.reshape(SEQS, KP * KP) / math.sqrt(TOK_SEQ)
    preconditioned = jnp.dot(sequence_grads, precondition, precision=lax.Precision.HIGHEST)
    rounded = preconditioned.astype(jnp.bfloat16)
    influence = jnp.dot(rounded, query_grads.T, preferred_element_type=jnp.float32) / math.sqrt(KP * KP)
    return influence
```

```python
import math

import jax
import jax.numpy as jnp
from jax import lax
from jax.sharding import PartitionSpec as P


def contract_last(left, right, precision=None):
    return lax.dot_general(
        left,
        right,
        (((1,), (1,)), ((), ())),
        precision=precision,
        preferred_element_type=jnp.float32,
    )


def swap(value, axis, bit):
    size = lax.axis_size(axis)
    return lax.ppermute(value, axis, [(i, i ^ bit) for i in range(size)])


def steps(size):
    return [1 << i for i in range(size.bit_length() - 1)]


def ordered(first, mine, other, axis):
    return jnp.where(
        first,
        jnp.concatenate((mine, other), axis),
        jnp.concatenate((other, mine), axis),
    )


def on_device(layer_input, gate_grad, factor_in, factor_out, precondition, query_grads):
    seq_length = layer_input.shape[0]
    own_rows, width = precondition.shape
    dp, dp_size = lax.axis_index("dp"), lax.axis_size("dp")
    core = lax.axis_index("tensor")

    inner = contract_last(factor_in, layer_input)
    inner_other = swap(inner, "tensor", 1)
    outer = contract_last(factor_out, gate_grad)
    outer_other = swap(outer, "tensor", 1)
    gradient = contract_last(
        inner + inner_other, outer + outer_other, lax.Precision.HIGHEST
    ) * (1 / math.sqrt(seq_length))

    blocks = gradient.reshape(dp_size, 2, own_rows)
    blocks = lax.dynamic_index_in_dim(blocks, core, 1, keepdims=False)[None]
    for bit in steps(dp_size):
        other = swap(blocks, "dp", bit)
        blocks = ordered((dp & bit) == 0, blocks, other, 0)
    col_block = lax.dynamic_index_in_dim(blocks, dp, 1, keepdims=False)

    partial = jnp.dot(col_block, precondition, precision=lax.Precision.HIGHEST)

    low, high = partial[:, : width // 2], partial[:, width // 2 :]
    given = jnp.where(core == 0, high, low)
    total = jnp.where(core == 0, low, high) + swap(given, "tensor", 1)
    for bit in steps(dp_size):
        total = total + swap(total, "dp", bit)

    rounded = total.astype(jnp.bfloat16)
    rounded = ordered(core == 0, rounded, swap(rounded, "tensor", 1), 1)
    return contract_last(rounded, query_grads) * (1 / math.sqrt(width))


def solution(mesh):
    in_specs = (
        P(("groups", "dp"), "tensor"),
        P(("groups", "dp"), "tensor"),
        P(None, "tensor"),
        P(None, "tensor"),
        P(("dp", "tensor"), None),
        P(("dp", "tensor"), None),
    )
    out_specs = P("groups", ("dp", "tensor"))
    return jax.shard_map(
        on_device, mesh=mesh, in_specs=in_specs, out_specs=out_specs, check_vma=False
    )
```

```python
import math

import jax
import jax.numpy as jnp
from jax import lax
from jax.experimental import pallas as pl
from jax.experimental.pallas import tpu as pltpu
from jax.sharding import PartitionSpec as P

CHUNK = 1024
BAND = 512
LAST = (((1,), (1,)), ((), ()))


def project_kernel(layer_ref, gate_ref, in_ref, out_ref, sides_ref, left, right, sems):
    rank = in_ref.shape[0]
    counts = (layer_ref.shape[1] // CHUNK, gate_ref.shape[1] // CHUNK)
    copies = []
    for part, (big, small) in enumerate(((layer_ref, in_ref), (gate_ref, out_ref))):
        for c in range(counts[part]):
            slot = len(copies)
            cols = pl.ds(c * CHUNK, CHUNK)
            copies.append(
                (
                    pltpu.make_async_copy(
                        small.at[:, cols],
                        right.at[slot, pl.ds(part * rank, rank)],
                        sems.at[0, slot],
                    ),
                    pltpu.make_async_copy(
                        big.at[:, cols], left.at[slot], sems.at[1, slot]
                    ),
                )
            )
    for pair in copies:
        for copy in pair:
            copy.start()
    blank = jnp.zeros((rank, CHUNK), right.dtype)
    for slot in range(len(copies)):
        right[slot, pl.ds(rank if slot < counts[0] else 0, rank)] = blank
    total = None
    for slot, pair in enumerate(copies):
        for copy in pair:
            copy.wait()
        term = lax.dot_general(
            left[slot], right[slot], LAST, preferred_element_type=jnp.float32
        )
        total = term if total is None else total + term
    sides_ref[...] = total


def project(layer_input, gate_grad, factor_in, factor_out):
    tokens, rank = layer_input.shape[0], factor_in.shape[0]
    features = layer_input.shape[1] + gate_grad.shape[1]
    slots = features // CHUNK
    return pl.pallas_call(
        project_kernel,
        out_shape=jax.ShapeDtypeStruct((tokens, 2 * rank), jnp.float32),
        in_specs=[pl.BlockSpec(memory_space=pl.ANY)] * 4,
        out_specs=pl.BlockSpec(memory_space=pltpu.VMEM),
        scratch_shapes=[
            pltpu.VMEM((slots, tokens, CHUNK), layer_input.dtype),
            pltpu.VMEM((slots, 2 * rank, CHUNK), factor_in.dtype),
            pltpu.SemaphoreType.DMA((2, slots)),
        ],
        compiler_params=pltpu.CompilerParams(vmem_limit_bytes=24 << 20),
        cost_estimate=pl.CostEstimate(
            flops=2 * tokens * features * rank,
            bytes_accessed=2 * (tokens + rank) * features,
            transcendentals=0,
        ),
        name="project",
    )(layer_input, gate_grad, factor_in, factor_out)


def split(value, terms):
    parts = []
    for _ in range(terms):
        part = value.astype(jnp.bfloat16)
        value = value - part.astype(jnp.float32)
        parts.append(part)
    return parts


def precondition_kernel(grads_ref, matrix_ref, result_ref):
    seqs = grads_ref.shape[0]
    grads = jnp.concatenate(split(grads_ref[...], 3), axis=0)
    width = matrix_ref.shape[1]
    for start in range(0, width, BAND):
        high, low = split(matrix_ref[:, start : start + BAND], 2)
        by_high = jnp.dot(grads, high, preferred_element_type=jnp.float32)
        by_low = jnp.dot(grads[: 2 * seqs], low, preferred_element_type=jnp.float32)
        small = by_high[2 * seqs :] + by_low[seqs:]
        middle = by_high[seqs : 2 * seqs] + by_low[:seqs]
        result_ref[:, start : start + BAND] = by_high[:seqs] + (middle + small)


def precondition_rows(grads, matrix):
    seqs, (rows, width) = grads.shape[0], matrix.shape
    return pl.pallas_call(
        precondition_kernel,
        out_shape=jax.ShapeDtypeStruct((seqs, width), jnp.float32),
        in_specs=[pl.BlockSpec(memory_space=pltpu.VMEM)] * 2,
        out_specs=pl.BlockSpec(memory_space=pltpu.VMEM),
        compiler_params=pltpu.CompilerParams(vmem_limit_bytes=24 << 20),
        cost_estimate=pl.CostEstimate(
            flops=2 * seqs * rows * width,
            bytes_accessed=4 * rows * width,
            transcendentals=0,
        ),
        name="precondition",
    )(grads, matrix)


def contract_last(left, right):
    return lax.dot_general(left, right, LAST, preferred_element_type=jnp.float32)


def swap(value, axis, bit):
    size = lax.axis_size(axis)
    return lax.ppermute(value, axis, [(i, i ^ bit) for i in range(size)])


def steps(size):
    return [1 << i for i in range(size.bit_length() - 1)]


def ordered(first, mine, other, axis):
    return jnp.where(
        first,
        jnp.concatenate((mine, other), axis),
        jnp.concatenate((other, mine), axis),
    )


def on_device(layer_input, gate_grad, factor_in, factor_out, precondition, query_grads):
    seq_length, rank = layer_input.shape[0], factor_in.shape[0]
    own_rows, width = precondition.shape
    dp, dp_size = lax.axis_index("dp"), lax.axis_size("dp")
    core = lax.axis_index("tensor")

    sides = project(layer_input, gate_grad, factor_in, factor_out)
    sides = sides + swap(sides, "tensor", 1)
    gradient = lax.dot_general(
        sides[:, :rank],
        sides[:, rank:],
        (((0,), (0,)), ((), ())),
        precision=lax.Precision.HIGHEST,
    ) * (1 / math.sqrt(seq_length))

    blocks = gradient.reshape(dp_size, 2, own_rows)
    blocks = lax.dynamic_index_in_dim(blocks, core, 1, keepdims=False)[None]
    for bit in steps(dp_size):
        other = swap(blocks, "dp", bit)
        blocks = ordered((dp & bit) == 0, blocks, other, 0)
    col_block = lax.dynamic_index_in_dim(blocks, dp, 1, keepdims=False)

    partial = precondition_rows(col_block, precondition)

    low, high = partial[:, : width // 2], partial[:, width // 2 :]
    given = jnp.where(core == 0, high, low)
    total = jnp.where(core == 0, low, high) + swap(given, "tensor", 1)
    for bit in steps(dp_size):
        total = total + swap(total, "dp", bit)

    rounded = total.astype(jnp.bfloat16)
    rounded = ordered(core == 0, rounded, swap(rounded, "tensor", 1), 1)
    return contract_last(rounded, query_grads) * (1 / math.sqrt(width))


def solution(mesh):
    in_specs = (
        P(("groups", "dp"), "tensor"),
        P(("groups", "dp"), "tensor"),
        P(None, "tensor"),
        P(None, "tensor"),
        P(("dp", "tensor"), None),
        P(("dp", "tensor"), None),
    )
    out_specs = P("groups", ("dp", "tensor"))
    return jax.shard_map(
        on_device, mesh=mesh, in_specs=in_specs, out_specs=out_specs, check_vma=False
    )
```

```python
import functools
import math

import jax
import jax.numpy as jnp
from jax import lax
from jax.experimental import pallas as pl
from jax.experimental.pallas import tpu as pltpu
from jax.sharding import PartitionSpec as P

CHUNK = 1024
BAND = 512
SHARES = (1, 1)
LAST = (((1,), (1,)), ((), ()))

ROUNDS_OF_8 = (
    ((1, 0, 4, 5, 2, 3, 7, 6), (3, 2, 6, 7, 0, 1, 5, 4)),
    ((2, 3, 0, 1, 6, 7, 4, 5), (3, 2, 6, 7, 0, 1, 5, 4)),
)


def gather_rounds(size):
    if size == 8:
        return [(pair, True) for pair in ROUNDS_OF_8]
    rounds = []
    for bit in steps(size):
        sources = tuple(i ^ bit for i in range(size))
        rounds.append(((sources, sources), False))
    return rounds


def gather_slots(size):
    held = [[[chip] for chip in range(size)] for _ in range(2)]
    for sources, swaps in gather_rounds(size):
        got = [[held[c][sources[c][i]] for i in range(size)] for c in range(2)]
        held = [
            [
                held[c][i] + got[c][i] + (got[1 - c][i] if swaps else [])
                for i in range(size)
            ]
            for c in range(2)
        ]
    return [[[row.index(s) for s in range(size)] for row in rows] for rows in held]


def packed(values, bits):
    word = sum(value << (bits * i) for i, value in enumerate(values))
    return word - (1 << 32) if word >= 1 << 31 else word


def unpacked(word, index, bits):
    return (word >> (bits * index)) & ((1 << bits) - 1)


def gather_target(sources, core, dp):
    size = len(sources[0])
    if size != 8:
        return dp ^ sources[0][0]
    words = [packed([row.index(i) for i in range(size)], 3) for row in sources]
    return unpacked(jnp.where(core == 0, words[0], words[1]), dp, 3)


def gather_slot(size):
    core, dp = lax.axis_index("tensor"), lax.axis_index("dp")
    if size != 8:
        return lambda s: dp ^ s
    place, word = core * size + dp, jnp.int32(0)
    for k, row in enumerate(sum(gather_slots(size), [])):
        word = jnp.where(place == k, jnp.int32(packed(row, 4)), word)
    return lambda s: unpacked(word, s, 4)


def project_kernel(layer_ref, gate_ref, in_ref, out_ref, sides_ref, left, right, sems):
    rank, tokens = in_ref.shape[0], layer_ref.shape[0]
    counts = (layer_ref.shape[1] // CHUNK, gate_ref.shape[1] // CHUNK)
    copies = []
    for part, (big, small) in enumerate(((layer_ref, in_ref), (gate_ref, out_ref))):
        for c in range(counts[part]):
            slot = len(copies)
            cols = pl.ds(c * CHUNK, CHUNK)
            copies.append(
                (
                    pltpu.make_async_copy(
                        small.at[:, cols],
                        right.at[slot, pl.ds(part * rank, rank)],
                        sems.at[0, slot],
                    ),
                    pltpu.make_async_copy(
                        big.at[:, cols], left.at[slot], sems.at[1, slot]
                    ),
                )
            )
    for pair in copies:
        for copy in pair:
            copy.start()
    blank = jnp.zeros((rank, CHUNK), right.dtype)
    for slot in range(len(copies)):
        right[slot, pl.ds(rank if slot < counts[0] else 0, rank)] = blank
    half = tokens // 2
    totals = [None, None]
    for slot, pair in enumerate(copies):
        for copy in pair:
            copy.wait()
        for h in range(2):
            term = lax.dot_general(
                left[slot, h * half : (h + 1) * half],
                right[slot],
                LAST,
                preferred_element_type=jnp.float32,
            )
            totals[h] = term if slot == 0 else totals[h] + term
    for h in range(2):
        sides_ref[h * half : (h + 1) * half] = totals[h]


def project(layer_input, gate_grad, factor_in, factor_out):
    tokens, rank = layer_input.shape[0], factor_in.shape[0]
    features = layer_input.shape[1] + gate_grad.shape[1]
    slots = features // CHUNK
    return pl.pallas_call(
        project_kernel,
        out_shape=jax.ShapeDtypeStruct((tokens, 2 * rank), jnp.float32),
        in_specs=[pl.BlockSpec(memory_space=pl.ANY)] * 4,
        out_specs=pl.BlockSpec(memory_space=pltpu.VMEM),
        scratch_shapes=[
            pltpu.VMEM((slots, tokens, CHUNK), layer_input.dtype),
            pltpu.VMEM((slots, 2 * rank, CHUNK), factor_in.dtype),
            pltpu.SemaphoreType.DMA((2, slots)),
        ],
        compiler_params=pltpu.CompilerParams(vmem_limit_bytes=54784 << 10),
        cost_estimate=pl.CostEstimate(
            flops=2 * tokens * features * rank,
            bytes_accessed=2 * (tokens + rank) * features,
            transcendentals=0,
        ),
        name="project",
    )(layer_input, gate_grad, factor_in, factor_out)


def bring_kernel(first, matrix_ref, *refs):
    band_ref, here_ref, sems = refs[-3:]
    copies = [
        pltpu.make_async_copy(
            matrix_ref.at[:, pl.ds(first + start, BAND)],
            band_ref.at[:, pl.ds(start, BAND)],
            sems.at[number],
        )
        for number, start in enumerate(range(0, band_ref.shape[1], BAND))
    ]
    for copy in copies:
        copy.start()
    here_ref[...] = jnp.zeros_like(here_ref)
    for copy in copies:
        copy.wait()


def bring(matrix, first, width, *after):
    rows = matrix.shape[0]
    return pl.pallas_call(
        lambda *refs: bring_kernel(first, *refs),
        out_shape=(
            jax.ShapeDtypeStruct((rows, width), matrix.dtype),
            jax.ShapeDtypeStruct((8, 128), jnp.float32),
        ),
        in_specs=[pl.BlockSpec(memory_space=pl.ANY)] * (1 + len(after)),
        out_specs=[pl.BlockSpec(memory_space=pltpu.VMEM)] * 2,
        scratch_shapes=[pltpu.SemaphoreType.DMA((width // BAND,))],
        compiler_params=pltpu.CompilerParams(vmem_limit_bytes=49 << 20),
        cost_estimate=pl.CostEstimate(
            flops=0, bytes_accessed=4 * rows * width, transcendentals=0
        ),
        name="bring",
    )(matrix, *after)


def split(value, terms):
    parts = []
    for _ in range(terms):
        part = value.astype(jnp.bfloat16)
        value = value - part.astype(jnp.float32)
        parts.append(part)
    return parts


def precondition_kernel(parts, token_ref, *refs):
    del token_ref
    *refs, result_ref, held = refs
    part_refs, bands = refs[:parts], refs[parts:]
    seqs, rows = result_ref.shape[0], held.shape[1]
    core, first = lax.axis_index("tensor"), 0
    for part_ref in part_refs:
        own = jnp.where(core == 0, part_ref[:, :rows], part_ref[:, rows:])
        held[first : first + part_ref.shape[0]] = own
        first += part_ref.shape[0]
    slot = gather_slot(seqs)
    grads = jnp.concatenate(
        [held[pl.ds(slot(s), 1), :] for s in range(seqs)], axis=0
    )
    grads = jnp.concatenate(split(grads, 3), axis=0)
    first = 0
    for band_ref in bands:
        for start in range(0, band_ref.shape[1], BAND):
            high, low = split(band_ref[:, start : start + BAND], 2)
            by_high = jnp.dot(grads, high, preferred_element_type=jnp.float32)
            by_low = jnp.dot(grads[: 2 * seqs], low, preferred_element_type=jnp.float32)
            small = by_high[2 * seqs :] + by_low[seqs:]
            middle = by_high[seqs : 2 * seqs] + by_low[:seqs]
            result_ref[:, first + start : first + start + BAND] = by_high[:seqs] + (
                middle + small
            )
        first += band_ref.shape[1]


def precondition_rows(parts, token, bands, seqs):
    rows, width = bands[0].shape[0], sum(band.shape[1] for band in bands)
    held = sum(part.shape[0] for part in parts)
    return pl.pallas_call(
        functools.partial(precondition_kernel, len(parts)),
        out_shape=jax.ShapeDtypeStruct((seqs, width), jnp.float32),
        in_specs=[pl.BlockSpec(memory_space=pl.ANY)]
        + [pl.BlockSpec(memory_space=pltpu.VMEM)] * (len(parts) + len(bands)),
        out_specs=pl.BlockSpec(memory_space=pltpu.VMEM),
        scratch_shapes=[pltpu.VMEM((held, rows), jnp.float32)],
        compiler_params=pltpu.CompilerParams(vmem_limit_bytes=16 << 20),
        cost_estimate=pl.CostEstimate(
            flops=2 * seqs * rows * width,
            bytes_accessed=4 * rows * width,
            transcendentals=0,
        ),
        name="precondition",
    )(token, *parts, *bands)


def contract_last(left, right):
    return lax.dot_general(left, right, LAST, preferred_element_type=jnp.float32)


def swap(value, axis, bit):
    size = lax.axis_size(axis)
    return lax.ppermute(value, axis, [(i, i ^ bit) for i in range(size)])


def receive(value, sources):
    pairs = [
        (2 * source + core, 2 * chip + core)
        for core in range(2)
        for chip, source in enumerate(sources[core])
    ]
    return lax.ppermute(value, ("dp", "tensor"), pairs)


def steps(size):
    return [1 << i for i in range(size.bit_length() - 1)]


def ordered(first, mine, other, axis):
    return jnp.where(
        first,
        jnp.concatenate((mine, other), axis),
        jnp.concatenate((other, mine), axis),
    )


def on_device(layer_input, gate_grad, factor_in, factor_out, precondition, query_grads):
    seq_length, rank = layer_input.shape[0], factor_in.shape[0]
    own_rows, width = precondition.shape
    dp, dp_size = lax.axis_index("dp"), lax.axis_size("dp")
    core = lax.axis_index("tensor")

    bands, tokens = [], []

    def beside(given, got):
        if len(bands) < len(SHARES):
            first = sum(band.shape[1] for band in bands)
            share = width * SHARES[len(bands)] // sum(SHARES)
            band, token = bring(precondition, first, share, given, *tokens[-1:])
            got, token = lax.optimization_barrier((got, token))
            bands.append(band)
            tokens.append(token)
        return got

    sides = project(layer_input, gate_grad, factor_in, factor_out)
    sides = sides + swap(sides, "tensor", 1)
    gradient = lax.dot_general(
        sides[:, :rank],
        sides[:, rank:],
        (((0,), (0,)), ((), ())),
        precision=lax.Precision.HIGHEST,
    ) * (1 / math.sqrt(seq_length))

    held = gradient.reshape(1, dp_size, 2 * own_rows)
    rounds = gather_rounds(dp_size)
    for number, (sources, swaps) in enumerate(rounds):
        given = held
        if number == len(rounds) - 1:
            target = gather_target(sources, core, dp)
            given = lax.dynamic_index_in_dim(held, target, 1, keepdims=False)
            held = lax.dynamic_index_in_dim(held, dp, 1, keepdims=False)
        got = beside(given, receive(given, sources))
        parts = [held, got] + ([swap(got, "tensor", 1)] if swaps else [])
        if number < len(rounds) - 1:
            held = jnp.concatenate(parts, axis=0)
    *parts, token = lax.optimization_barrier((*parts, tokens[-1]))

    partial = precondition_rows(parts, token, bands, dp_size)

    low, high = partial[:, : width // 2], partial[:, width // 2 :]
    given = jnp.where(core == 0, high, low)
    total = jnp.where(core == 0, low, high) + swap(given, "tensor", 1)
    for bit in steps(dp_size):
        total = total + swap(total, "dp", bit)

    rounded = total.astype(jnp.bfloat16)
    rounded = ordered(core == 0, rounded, swap(rounded, "tensor", 1), 1)
    return contract_last(rounded, query_grads) * (1 / math.sqrt(width))


def solution(mesh):
    in_specs = (
        P(("groups", "dp"), "tensor"),
        P(("groups", "dp"), "tensor"),
        P(None, "tensor"),
        P(None, "tensor"),
        P(("dp", "tensor"), None),
        P(("dp", "tensor"), None),
    )
    out_specs = P("groups", ("dp", "tensor"))
    return jax.shard_map(
        on_device, mesh=mesh, in_specs=in_specs, out_specs=out_specs, check_vma=False
    )
```

```python
import functools
import math

import jax
import jax.numpy as jnp
from jax import lax
from jax.experimental import pallas as pl
from jax.experimental.pallas import tpu as pltpu
from jax.sharding import PartitionSpec as P

CHUNK = 1024
BAND = 512
BESIDE = 128
SHARES = (1, 1, 2)
LAST = (((1,), (1,)), ((), ()))

ROUNDS_OF_8 = (
    ((2, 3, 0, 1, 6, 7, 4, 5), (4, 5, 1, 0, 7, 6, 2, 3)),
    ((1, 0, 4, 5, 2, 3, 7, 6), (4, 5, 1, 0, 7, 6, 2, 3)),
)


def gather_rounds(size):
    if size == 8:
        return [(pair, True) for pair in ROUNDS_OF_8]
    rounds = []
    for bit in steps(size):
        sources = tuple(i ^ bit for i in range(size))
        rounds.append(((sources, sources), False))
    return rounds


def gather_slots(size):
    held = [[[chip] for chip in range(size)] for _ in range(2)]
    for sources, swaps in gather_rounds(size):
        got = [[held[c][sources[c][i]] for i in range(size)] for c in range(2)]
        held = [
            [
                held[c][i] + got[c][i] + (got[1 - c][i] if swaps else [])
                for i in range(size)
            ]
            for c in range(2)
        ]
    return [[[row.index(s) for s in range(size)] for row in rows] for rows in held]


def packed(values, bits):
    word = sum(value << (bits * i) for i, value in enumerate(values))
    return word - (1 << 32) if word >= 1 << 31 else word


def unpacked(word, index, bits):
    return (word >> (bits * index)) & ((1 << bits) - 1)


def gather_target(sources, core, dp):
    size = len(sources[0])
    if size != 8:
        return dp ^ sources[0][0]
    words = [packed([row.index(i) for i in range(size)], 3) for row in sources]
    return unpacked(jnp.where(core == 0, words[0], words[1]), dp, 3)


def gather_slot(size):
    core, dp = lax.axis_index("tensor"), lax.axis_index("dp")
    if size != 8:
        return lambda s: dp ^ s
    place, word = core * size + dp, jnp.int32(0)
    for k, row in enumerate(sum(gather_slots(size), [])):
        word = jnp.where(place == k, jnp.int32(packed(row, 4)), word)
    return lambda s: unpacked(word, s, 4)


def project_kernel(layer_ref, gate_ref, in_ref, out_ref, sides_ref, left, right, sems):
    rank, tokens = in_ref.shape[0], layer_ref.shape[0]
    counts = (layer_ref.shape[1] // CHUNK, gate_ref.shape[1] // CHUNK)
    copies = []
    for part, (big, small) in enumerate(((layer_ref, in_ref), (gate_ref, out_ref))):
        for c in range(counts[part]):
            slot = len(copies)
            cols = pl.ds(c * CHUNK, CHUNK)
            copies.append(
                (
                    pltpu.make_async_copy(
                        small.at[:, cols],
                        right.at[slot, pl.ds(part * rank, rank)],
                        sems.at[0, slot],
                    ),
                    pltpu.make_async_copy(
                        big.at[:, cols], left.at[slot], sems.at[1, slot]
                    ),
                )
            )
    for pair in copies:
        for copy in pair:
            copy.start()
    blank = jnp.zeros((rank, CHUNK), right.dtype)
    for slot in range(len(copies)):
        right[slot, pl.ds(rank if slot < counts[0] else 0, rank)] = blank
    half = tokens // 2
    totals = [None, None]
    for slot, pair in enumerate(copies):
        for copy in pair:
            copy.wait()
        for h in range(2):
            term = lax.dot_general(
                left[slot, h * half : (h + 1) * half],
                right[slot],
                LAST,
                preferred_element_type=jnp.float32,
            )
            totals[h] = term if slot == 0 else totals[h] + term
    for h in range(2):
        sides_ref[h * half : (h + 1) * half] = totals[h]


def project(layer_input, gate_grad, factor_in, factor_out):
    tokens, rank = layer_input.shape[0], factor_in.shape[0]
    features = layer_input.shape[1] + gate_grad.shape[1]
    slots = features // CHUNK
    return pl.pallas_call(
        project_kernel,
        out_shape=jax.ShapeDtypeStruct((tokens, 2 * rank), jnp.float32),
        in_specs=[pl.BlockSpec(memory_space=pl.ANY)] * 4,
        out_specs=pl.BlockSpec(memory_space=pltpu.VMEM),
        scratch_shapes=[
            pltpu.VMEM((slots, tokens, CHUNK), layer_input.dtype),
            pltpu.VMEM((slots, 2 * rank, CHUNK), factor_in.dtype),
            pltpu.SemaphoreType.DMA((2, slots)),
        ],
        compiler_params=pltpu.CompilerParams(vmem_limit_bytes=54784 << 10),
        cost_estimate=pl.CostEstimate(
            flops=2 * tokens * features * rank,
            bytes_accessed=2 * (tokens + rank) * features,
            transcendentals=0,
        ),
        name="project",
    )(layer_input, gate_grad, factor_in, factor_out)


def gradient_kernel(mine_ref, other_ref, result_ref, square):
    tokens, rank = mine_ref.shape[0], square.shape[0]
    terms = jnp.concatenate(split(mine_ref[...] + other_ref[...], 3), axis=1)
    product = lax.dot_general(
        terms, terms, (((0,), (0,)), ((), ())), preferred_element_type=jnp.float32
    )

    def block(i, j):
        rows = product[2 * rank * i : 2 * rank * i + rank]
        return rows[:, 2 * rank * j : 2 * rank * (j + 1)]

    small = block(0, 2) + block(2, 0) + block(1, 1)
    full = block(0, 0) + (block(0, 1) + block(1, 0) + small)
    square[...] = full[:, rank:] * (1 / math.sqrt(tokens))
    rows = result_ref.shape[0]
    each = rank // rows
    for k in range(each):
        result_ref[:, k * rank : (k + 1) * rank] = square[pl.ds(k, rows, each), :]


def gradient_rows(mine, other, rows):
    tokens, rank = mine.shape[0], mine.shape[1] // 2
    return pl.pallas_call(
        gradient_kernel,
        out_shape=jax.ShapeDtypeStruct((rows, rank * rank // rows), jnp.float32),
        in_specs=[pl.BlockSpec(memory_space=pltpu.VMEM)] * 2,
        out_specs=pl.BlockSpec(memory_space=pltpu.VMEM),
        scratch_shapes=[pltpu.VMEM((rank, rank), jnp.float32)],
        compiler_params=pltpu.CompilerParams(vmem_limit_bytes=16 << 20),
        cost_estimate=pl.CostEstimate(
            flops=2 * tokens * rank * rank,
            bytes_accessed=16 * tokens * rank,
            transcendentals=0,
        ),
        name="gradient",
    )(mine, other)


def bring_kernel(first, matrix_ref, *refs):
    band_ref, here_ref, sems = refs[-3:]
    copies = [
        pltpu.make_async_copy(
            matrix_ref.at[:, pl.ds(first + start, BAND)],
            band_ref.at[:, pl.ds(start, BAND)],
            sems.at[number],
        )
        for number, start in enumerate(range(0, band_ref.shape[1], BAND))
    ]
    for copy in copies:
        copy.start()
    here_ref[...] = jnp.zeros_like(here_ref)
    for copy in copies:
        copy.wait()


def bring(matrix, first, width, *after):
    rows = matrix.shape[0]
    return pl.pallas_call(
        lambda *refs: bring_kernel(first, *refs),
        out_shape=(
            jax.ShapeDtypeStruct((rows, width), matrix.dtype),
            jax.ShapeDtypeStruct((8, 128), jnp.float32),
        ),
        in_specs=[pl.BlockSpec(memory_space=pl.ANY)] * (1 + len(after)),
        out_specs=[pl.BlockSpec(memory_space=pltpu.VMEM)] * 2,
        scratch_shapes=[pltpu.SemaphoreType.DMA((width // BAND,))],
        compiler_params=pltpu.CompilerParams(vmem_limit_bytes=49 << 20),
        cost_estimate=pl.CostEstimate(
            flops=0, bytes_accessed=4 * rows * width, transcendentals=0
        ),
        name="bring",
    )(matrix, *after)


def split(value, terms):
    parts = []
    for _ in range(terms):
        part = value.astype(jnp.bfloat16)
        value = value - part.astype(jnp.float32)
        parts.append(part)
    return parts


def precondition_kernel(parts, token_ref, *refs):
    del token_ref
    *refs, result_ref, held = refs
    part_refs, bands = refs[:parts], refs[parts:]
    seqs, rows = result_ref.shape[0], held.shape[1]
    core, first = lax.axis_index("tensor"), 0
    for part_ref in part_refs:
        own = jnp.where(core == 0, part_ref[:, :rows], part_ref[:, rows:])
        held[first : first + part_ref.shape[0]] = own
        first += part_ref.shape[0]
    slot = gather_slot(seqs)
    grads = jnp.concatenate(
        [held[pl.ds(slot(s), 1), :] for s in range(seqs)], axis=0
    )
    grads = jnp.concatenate(split(grads, 3), axis=0)
    first = 0
    for band_ref in bands:
        for start in range(0, band_ref.shape[1], BAND):
            high, low = split(band_ref[:, start : start + BAND], 2)
            by_high = jnp.dot(grads, high, preferred_element_type=jnp.float32)
            by_low = jnp.dot(grads[: 2 * seqs], low, preferred_element_type=jnp.float32)
            small = by_high[2 * seqs :] + by_low[seqs:]
            middle = by_high[seqs : 2 * seqs] + by_low[:seqs]
            result_ref[:, first + start : first + start + BAND] = by_high[:seqs] + (
                middle + small
            )
        first += band_ref.shape[1]
    top = jnp.max(jnp.abs(result_ref[:, :first]), axis=1, keepdims=True)
    power = jnp.floor(jnp.log2(jnp.clip(top, 1e-30, 1e30))) - 14
    result_ref[:, first:] = jnp.broadcast_to(power, (seqs, BESIDE))


def precondition_rows(parts, token, bands, seqs):
    rows, width = bands[0].shape[0], sum(band.shape[1] for band in bands)
    held = sum(part.shape[0] for part in parts)
    return pl.pallas_call(
        functools.partial(precondition_kernel, len(parts)),
        out_shape=jax.ShapeDtypeStruct((seqs, width + BESIDE), jnp.float32),
        in_specs=[pl.BlockSpec(memory_space=pl.ANY)]
        + [pl.BlockSpec(memory_space=pltpu.VMEM)] * (len(parts) + len(bands)),
        out_specs=pl.BlockSpec(memory_space=pltpu.VMEM),
        scratch_shapes=[pltpu.VMEM((held, rows), jnp.float32)],
        compiler_params=pltpu.CompilerParams(vmem_limit_bytes=16 << 20),
        cost_estimate=pl.CostEstimate(
            flops=2 * seqs * rows * width,
            bytes_accessed=4 * rows * width,
            transcendentals=0,
        ),
        name="precondition",
    )(token, *parts, *bands)


def contract_last(left, right):
    return lax.dot_general(left, right, LAST, preferred_element_type=jnp.float32)


def swap(value, axis, bit):
    size = lax.axis_size(axis)
    return lax.ppermute(value, axis, [(i, i ^ bit) for i in range(size)])


def receive(value, sources):
    pairs = [
        (2 * source + core, 2 * chip + core)
        for core in range(2)
        for chip, source in enumerate(sources[core])
    ]
    return lax.ppermute(value, ("dp", "tensor"), pairs)


def flip(value, steps):
    size = lax.axis_size("dp")
    pairs = []
    for place in range(2 * size):
        family = (place ^ odd(place >> 1)) & 1
        pairs.append((place, place ^ (2 * steps[family] + 1)))
    return lax.ppermute(value, ("dp", "tensor"), pairs)


def odd(number):
    for shift in (8, 4, 2, 1):
        number = number ^ (number >> shift)
    return number & 1


def steps(size):
    return [1 << i for i in range(size.bit_length() - 1)]


def ordered(first, mine, other, axis):
    return jnp.where(
        first,
        jnp.concatenate((mine, other), axis),
        jnp.concatenate((other, mine), axis),
    )


def add_cores_kernel(mine_ref, other_ref, sum_ref, code_ref):
    width = sum_ref.shape[1] - BESIDE
    power = jnp.maximum(mine_ref[:, width:], other_ref[:, width:]) + 1
    scale = jnp.exp2(-power)
    for start in range(0, width, BESIDE):
        lanes = slice(start, start + BESIDE)
        total = mine_ref[:, lanes] + other_ref[:, lanes]
        sum_ref[:, lanes] = total
        code_ref[:, lanes] = total * scale
    sum_ref[:, width:] = power
    code_ref[:, width:] = power


def add_first_kernel(mine_ref, got_ref, swapped_ref, sum_ref, code_ref):
    width = sum_ref.shape[1]
    powers = [ref[:, width:] for ref in (mine_ref, got_ref, swapped_ref)]
    power = jnp.maximum(jnp.maximum(powers[0], powers[1]), powers[2]) + 2
    got_scale, swapped_scale = jnp.exp2(powers[1]), jnp.exp2(powers[2])
    scale = jnp.exp2(-power)
    own = jnp.where(lax.axis_index("tensor") == 0, 1.0, 0.0)
    for start in range(0, width, BESIDE):
        lanes = slice(start, start + BESIDE)
        first = got_ref[:, lanes] * got_scale + swapped_ref[:, lanes] * swapped_scale
        mine = mine_ref[:, lanes]
        sum_ref[:, lanes] = mine + first
        code_ref[:, lanes] = (first + mine * own) * scale
    code_ref[:, width:] = power


def score_kernel(sum_ref, got_ref, swapped_ref, query_ref, result_ref, rounded):
    width = sum_ref.shape[1]
    got_scale = jnp.exp2(got_ref[:, width:])
    swapped_scale = jnp.exp2(swapped_ref[:, width:])
    for start in range(0, width, BESIDE):
        lanes = slice(start, start + BESIDE)
        second = got_ref[:, lanes] * got_scale + swapped_ref[:, lanes] * swapped_scale
        rounded[:, lanes] = (sum_ref[:, lanes] + second).astype(rounded.dtype)
    step = width // 4
    total = sum(
        contract_last(
            rounded[:, start : start + step], query_ref[:, start : start + step]
        )
        for start in range(0, width, step)
    )
    result_ref[...] = total * (1 / math.sqrt(width))


def small_kernel(kernel, name, operands, shapes, scratch=()):
    return pl.pallas_call(
        kernel,
        out_shape=[jax.ShapeDtypeStruct(shape, jnp.float32) for shape in shapes],
        in_specs=[pl.BlockSpec(memory_space=pltpu.VMEM)] * len(operands),
        out_specs=[pl.BlockSpec(memory_space=pltpu.VMEM)] * len(shapes),
        scratch_shapes=scratch,
        compiler_params=pltpu.CompilerParams(vmem_limit_bytes=16 << 20),
        name=name,
    )(*operands)


def score_by_rounds(partial, query_grads):
    def heard(code, sources):
        got = receive(code.astype(jnp.float16), sources)
        swapped = swap(got, "tensor", 1)
        return got.astype(jnp.float32), swapped.astype(jnp.float32)

    seqs, extent = partial.shape
    wide, narrow = (seqs, extent), (seqs, extent - BESIDE)
    other = swap(partial, "tensor", 1)
    mine, code = small_kernel(
        add_cores_kernel, "add_cores", (partial, other), (wide, wide)
    )
    heard_first = heard(code, ROUNDS_OF_8[0])
    total, code = small_kernel(
        add_first_kernel, "add_first", (mine, *heard_first), (narrow, wide)
    )
    heard_second = heard(code, ROUNDS_OF_8[1])
    return small_kernel(
        score_kernel,
        "score",
        (total, *heard_second, query_grads),
        ((seqs, query_grads.shape[0]),),
        [pltpu.VMEM(narrow, jnp.bfloat16)],
    )[0]


def add_steps(partial):
    half = (partial.shape[1] - BESIDE) // 2
    even = lax.axis_index("tensor") == odd(lax.axis_index("dp"))
    low, high = partial[:, :half], partial[:, half : 2 * half]
    given = jnp.where(even, high, low)
    total = jnp.where(even, low, high) + swap(given, "tensor", 1)
    bits = steps(lax.axis_size("dp"))
    for pair in zip(bits, bits[::-1]):
        total = total + flip(total, pair)
    return ordered(even, total, swap(total, "tensor", 1), 1)


def on_device(layer_input, gate_grad, factor_in, factor_out, precondition, query_grads):
    own_rows, width = precondition.shape
    dp, dp_size = lax.axis_index("dp"), lax.axis_size("dp")
    core = lax.axis_index("tensor")

    bands, tokens = [], []

    def beside(given, got):
        if len(bands) < len(SHARES):
            first = sum(band.shape[1] for band in bands)
            share = width * SHARES[len(bands)] // sum(SHARES)
            band, token = bring(precondition, first, share, given, *tokens[-1:])
            got, token = lax.optimization_barrier((got, token))
            bands.append(band)
            tokens.append(token)
        return got

    sides = project(layer_input, gate_grad, factor_in, factor_out)
    other = beside(sides, swap(sides, "tensor", 1))
    gradient = gradient_rows(sides, other, dp_size)

    held = gradient[None]
    rounds = gather_rounds(dp_size)
    for number, (sources, swaps) in enumerate(rounds):
        given = held
        if number == len(rounds) - 1:
            target = gather_target(sources, core, dp)
            given = lax.dynamic_index_in_dim(held, target, 1, keepdims=False)
            held = lax.dynamic_index_in_dim(held, dp, 1, keepdims=False)
        got = beside(given, receive(given, sources))
        parts = [held, got] + ([swap(got, "tensor", 1)] if swaps else [])
        if number < len(rounds) - 1:
            held = jnp.concatenate(parts, axis=0)
    *parts, token = lax.optimization_barrier((*parts, tokens[-1]))

    partial = precondition_rows(parts, token, bands, dp_size)

    if dp_size == 8:
        return score_by_rounds(partial, query_grads)
    rounded = add_steps(partial).astype(jnp.bfloat16)
    return contract_last(rounded, query_grads) * (1 / math.sqrt(width))


def solution(mesh):
    in_specs = (
        P(("groups", "dp"), "tensor"),
        P(("groups", "dp"), "tensor"),
        P(None, "tensor"),
        P(None, "tensor"),
        P(("dp", "tensor"), None),
        P(("dp", "tensor"), None),
    )
    out_specs = P("groups", ("dp", "tensor"))
    return jax.shard_map(
        on_device, mesh=mesh, in_specs=in_specs, out_specs=out_specs, check_vma=False
    )
```

```python
import functools
import math

import jax
import jax.numpy as jnp
from jax import lax
from jax.experimental import pallas as pl
from jax.experimental.pallas import tpu as pltpu
from jax.sharding import PartitionSpec as P

CHUNK = 1024
BAND = 512
BESIDE = 128
LAST = (((1,), (1,)), ((), ()))

ROUNDS_OF_8 = (
    ((2, 3, 0, 1, 6, 7, 4, 5), (4, 5, 1, 0, 7, 6, 2, 3)),
    ((1, 0, 4, 5, 2, 3, 7, 6), (4, 5, 1, 0, 7, 6, 2, 3)),
)


def gather_rounds(size):
    if size == 8:
        return [(pair, True) for pair in ROUNDS_OF_8]
    rounds = []
    for bit in steps(size):
        sources = tuple(i ^ bit for i in range(size))
        rounds.append(((sources, sources), False))
    return rounds


def gather_slots(size):
    held = [[[chip] for chip in range(size)] for _ in range(2)]
    for sources, swaps in gather_rounds(size):
        got = [[held[c][sources[c][i]] for i in range(size)] for c in range(2)]
        held = [
            [
                held[c][i] + got[c][i] + (got[1 - c][i] if swaps else [])
                for i in range(size)
            ]
            for c in range(2)
        ]
    return [[[row.index(s) for s in range(size)] for row in rows] for rows in held]


def packed(values, bits):
    word = sum(value << (bits * i) for i, value in enumerate(values))
    return word - (1 << 32) if word >= 1 << 31 else word


def unpacked(word, index, bits):
    return (word >> (bits * index)) & ((1 << bits) - 1)


def gather_target(sources, core, dp):
    size = len(sources[0])
    if size != 8:
        return dp ^ sources[0][0]
    words = [packed([row.index(i) for i in range(size)], 3) for row in sources]
    return unpacked(jnp.where(core == 0, words[0], words[1]), dp, 3)


def gather_slot(size):
    core, dp = lax.axis_index("tensor"), lax.axis_index("dp")
    if size != 8:
        return lambda s: dp ^ s
    place, word = core * size + dp, jnp.int32(0)
    for k, row in enumerate(sum(gather_slots(size), [])):
        word = jnp.where(place == k, jnp.int32(packed(row, 4)), word)
    return lambda s: unpacked(word, s, 4)


def project_kernel(layer_ref, gate_ref, in_ref, out_ref, sides_ref, left, right, sems):
    rank, tokens = in_ref.shape[0], layer_ref.shape[0]
    counts = (layer_ref.shape[1] // CHUNK, gate_ref.shape[1] // CHUNK)
    copies = []
    for part, (big, small) in enumerate(((layer_ref, in_ref), (gate_ref, out_ref))):
        for c in range(counts[part]):
            slot = len(copies)
            cols = pl.ds(c * CHUNK, CHUNK)
            copies.append(
                (
                    pltpu.make_async_copy(
                        small.at[:, cols],
                        right.at[slot, pl.ds(part * rank, rank)],
                        sems.at[0, slot],
                    ),
                    pltpu.make_async_copy(
                        big.at[:, cols], left.at[slot], sems.at[1, slot]
                    ),
                )
            )
    for pair in copies:
        for copy in pair:
            copy.start()
    blank = jnp.zeros((rank, CHUNK), right.dtype)
    for slot in range(len(copies)):
        right[slot, pl.ds(rank if slot < counts[0] else 0, rank)] = blank
    half = tokens // 2
    totals = [None, None]
    for slot, pair in enumerate(copies):
        for copy in pair:
            copy.wait()
        for h in range(2):
            term = lax.dot_general(
                left[slot, h * half : (h + 1) * half],
                right[slot],
                LAST,
                preferred_element_type=jnp.float32,
            )
            totals[h] = term if slot == 0 else totals[h] + term
    for h in range(2):
        sides_ref[h * half : (h + 1) * half] = totals[h]


def project(layer_input, gate_grad, factor_in, factor_out):
    tokens, rank = layer_input.shape[0], factor_in.shape[0]
    features = layer_input.shape[1] + gate_grad.shape[1]
    slots = features // CHUNK
    return pl.pallas_call(
        project_kernel,
        out_shape=jax.ShapeDtypeStruct((tokens, 2 * rank), jnp.float32),
        in_specs=[pl.BlockSpec(memory_space=pl.ANY)] * 4,
        out_specs=pl.BlockSpec(memory_space=pltpu.VMEM),
        scratch_shapes=[
            pltpu.VMEM((slots, tokens, CHUNK), layer_input.dtype),
            pltpu.VMEM((slots, 2 * rank, CHUNK), factor_in.dtype),
            pltpu.SemaphoreType.DMA((2, slots)),
        ],
        compiler_params=pltpu.CompilerParams(vmem_limit_bytes=54784 << 10),
        cost_estimate=pl.CostEstimate(
            flops=2 * tokens * features * rank,
            bytes_accessed=2 * (tokens + rank) * features,
            transcendentals=0,
        ),
        name="project",
    )(layer_input, gate_grad, factor_in, factor_out)


def gradient_kernel(mine_ref, other_ref, result_ref, square):
    tokens, rank = mine_ref.shape[0], square.shape[0]
    terms = jnp.concatenate(split(mine_ref[...] + other_ref[...], 2), axis=1)
    product = lax.dot_general(
        terms, terms, (((0,), (0,)), ((), ())), preferred_element_type=jnp.float32
    )

    def block(i, j):
        rows = product[2 * rank * i : 2 * rank * i + rank]
        return rows[:, 2 * rank * j : 2 * rank * (j + 1)]

    full = block(0, 0) + (block(0, 1) + block(1, 0) + block(1, 1))
    square[...] = full[:, rank:] * (1 / math.sqrt(tokens))
    rows = result_ref.shape[0]
    each = rank // rows
    for k in range(each):
        result_ref[:, k * rank : (k + 1) * rank] = square[pl.ds(k, rows, each), :]


def gradient_rows(mine, other, rows):
    tokens, rank = mine.shape[0], mine.shape[1] // 2
    return pl.pallas_call(
        gradient_kernel,
        out_shape=jax.ShapeDtypeStruct((rows, rank * rank // rows), jnp.float32),
        in_specs=[pl.BlockSpec(memory_space=pltpu.VMEM)] * 2,
        out_specs=pl.BlockSpec(memory_space=pltpu.VMEM),
        scratch_shapes=[pltpu.VMEM((rank, rank), jnp.float32)],
        compiler_params=pltpu.CompilerParams(vmem_limit_bytes=16 << 20),
        cost_estimate=pl.CostEstimate(
            flops=2 * tokens * rank * rank,
            bytes_accessed=16 * tokens * rank,
            transcendentals=0,
        ),
        name="gradient",
    )(mine, other)


def split(value, terms):
    parts = []
    for _ in range(terms):
        part = value.astype(jnp.bfloat16)
        value = value - part.astype(jnp.float32)
        parts.append(part)
    return parts


def pack_kernel(sources, *refs):
    *held_refs, given_ref, kept_ref = refs
    core, dp = lax.axis_index("tensor"), lax.axis_index("dp")
    target = gather_target(sources, core, dp)
    for row, ref in enumerate(held_refs):
        given_ref[row : row + 1] = ref[pl.ds(target, 1), :]
        kept_ref[row : row + 1] = ref[pl.ds(dp, 1), :]


def pack(held, sources):
    return pl.pallas_call(
        functools.partial(pack_kernel, sources),
        out_shape=[jax.ShapeDtypeStruct((len(held), held[0].shape[1]), jnp.float32)] * 2,
        in_specs=[pl.BlockSpec(memory_space=pltpu.VMEM)] * len(held),
        out_specs=[pl.BlockSpec(memory_space=pltpu.VMEM)] * 2,
        compiler_params=pltpu.CompilerParams(vmem_limit_bytes=16 << 20),
        name="pack",
    )(*held)


def split_kernel(after_ref, *refs):
    del after_ref
    *bands, high_ref, low_ref = refs
    first = 0
    for band_ref in bands:
        for start in range(0, band_ref.shape[1], BAND):
            lanes = slice(first + start, first + start + BAND)
            high_ref[:, lanes], low_ref[:, lanes] = split(
                band_ref[:, start : start + BAND], 2
            )
        first += band_ref.shape[1]


def split_bands(bands, after):
    shape = (bands[0].shape[0], sum(band.shape[1] for band in bands))
    return pl.pallas_call(
        split_kernel,
        out_shape=[jax.ShapeDtypeStruct(shape, jnp.bfloat16)] * 2,
        in_specs=[pl.BlockSpec(memory_space=pl.ANY)]
        + [pl.BlockSpec(memory_space=pltpu.VMEM)] * len(bands),
        out_specs=[pl.BlockSpec(memory_space=pltpu.VMEM)] * 2,
        compiler_params=pltpu.CompilerParams(vmem_limit_bytes=16 << 20),
        cost_estimate=pl.CostEstimate(
            flops=0, bytes_accessed=8 * shape[0] * shape[1], transcendentals=0
        ),
        name="split",
    )(after, *bands)


def precondition_kernel(token_ref, *refs):
    del token_ref
    *refs, result_ref, held = refs
    *part_refs, high_ref, low_ref = refs
    seqs, rows = result_ref.shape[0], held.shape[1]
    core, first = lax.axis_index("tensor"), 0
    for part_ref in part_refs:
        own = jnp.where(core == 0, part_ref[:, :rows], part_ref[:, rows:])
        held[first : first + part_ref.shape[0]] = own
        first += part_ref.shape[0]
    slot = gather_slot(seqs)
    grads = jnp.concatenate(
        [held[pl.ds(slot(s), 1), :] for s in range(seqs)], axis=0
    )
    grads = jnp.concatenate(split(grads, 2), axis=0)
    width = high_ref.shape[1]
    for start in range(0, width, BAND):
        lanes = slice(start, start + BAND)
        by_high, by_low = (
            jnp.dot(grads, ref[:, lanes], preferred_element_type=jnp.float32)
            for ref in (high_ref, low_ref)
        )
        small = by_high[seqs:] + by_low[:seqs] + by_low[seqs:]
        result_ref[:, lanes] = by_high[:seqs] + small
    top = jnp.max(jnp.abs(result_ref[:, :width]), axis=1, keepdims=True)
    power = jnp.floor(jnp.log2(jnp.clip(top, 1e-30, 1e30))) - 14
    result_ref[:, width:] = jnp.broadcast_to(power, (seqs, BESIDE))


def precondition_rows(parts, token, matrices, seqs):
    rows, width = matrices[0].shape
    held = sum(part.shape[0] for part in parts)
    return pl.pallas_call(
        precondition_kernel,
        out_shape=jax.ShapeDtypeStruct((seqs, width + BESIDE), jnp.float32),
        in_specs=[pl.BlockSpec(memory_space=pl.ANY)]
        + [pl.BlockSpec(memory_space=pltpu.VMEM)] * (len(parts) + len(matrices)),
        out_specs=pl.BlockSpec(memory_space=pltpu.VMEM),
        scratch_shapes=[pltpu.VMEM((held, rows), jnp.float32)],
        compiler_params=pltpu.CompilerParams(vmem_limit_bytes=16 << 20),
        cost_estimate=pl.CostEstimate(
            flops=2 * seqs * rows * width,
            bytes_accessed=4 * rows * width,
            transcendentals=0,
        ),
        name="precondition",
    )(token, *parts, *matrices)


def contract_last(left, right):
    return lax.dot_general(left, right, LAST, preferred_element_type=jnp.float32)


def swap(value, axis, bit):
    size = lax.axis_size(axis)
    return lax.ppermute(value, axis, [(i, i ^ bit) for i in range(size)])


def receive(value, sources, across=0):
    pairs = [
        (2 * source + (core ^ across), 2 * chip + core)
        for core in range(2)
        for chip, source in enumerate(sources[core])
    ]
    return lax.ppermute(value, ("dp", "tensor"), pairs)


def flip(value, steps):
    size = lax.axis_size("dp")
    pairs = []
    for place in range(2 * size):
        family = (place ^ odd(place >> 1)) & 1
        pairs.append((place, place ^ (2 * steps[family] + 1)))
    return lax.ppermute(value, ("dp", "tensor"), pairs)


def odd(number):
    for shift in (8, 4, 2, 1):
        number = number ^ (number >> shift)
    return number & 1


def steps(size):
    return [1 << i for i in range(size.bit_length() - 1)]


def ordered(first, mine, other, axis):
    return jnp.where(
        first,
        jnp.concatenate((mine, other), axis),
        jnp.concatenate((other, mine), axis),
    )


def add_cores_kernel(mine_ref, other_ref, sum_ref, code_ref):
    width = sum_ref.shape[1] - BESIDE
    power = jnp.maximum(mine_ref[:, width:], other_ref[:, width:]) + 1
    scale = jnp.exp2(-power)
    for start in range(0, width, BESIDE):
        lanes = slice(start, start + BESIDE)
        total = mine_ref[:, lanes] + other_ref[:, lanes]
        sum_ref[:, lanes] = total
        code_ref[:, lanes] = total * scale
    sum_ref[:, width:] = power
    code_ref[:, width:] = power


def add_first_kernel(mine_ref, got_ref, swapped_ref, sum_ref, code_ref):
    width = sum_ref.shape[1]
    powers = [ref[:, width:] for ref in (mine_ref, got_ref, swapped_ref)]
    power = jnp.maximum(jnp.maximum(powers[0], powers[1]), powers[2]) + 2
    got_scale, swapped_scale = jnp.exp2(powers[1]), jnp.exp2(powers[2])
    scale = jnp.exp2(-power)
    own = jnp.where(lax.axis_index("tensor") == 0, 1.0, 0.0)
    for start in range(0, width, BESIDE):
        lanes = slice(start, start + BESIDE)
        first = got_ref[:, lanes] * got_scale + swapped_ref[:, lanes] * swapped_scale
        mine = mine_ref[:, lanes]
        sum_ref[:, lanes] = mine + first
        code_ref[:, lanes] = (first + mine * own) * scale
    code_ref[:, width:] = power


def score_kernel(sum_ref, got_ref, swapped_ref, query_ref, result_ref, rounded):
    width = sum_ref.shape[1]
    got_scale = jnp.exp2(got_ref[:, width:])
    swapped_scale = jnp.exp2(swapped_ref[:, width:])
    for start in range(0, width, BESIDE):
        lanes = slice(start, start + BESIDE)
        second = got_ref[:, lanes] * got_scale + swapped_ref[:, lanes] * swapped_scale
        rounded[:, lanes] = (sum_ref[:, lanes] + second).astype(rounded.dtype)
    step = width // 4
    total = sum(
        contract_last(
            rounded[:, start : start + step], query_ref[:, start : start + step]
        )
        for start in range(0, width, step)
    )
    result_ref[...] = total * (1 / math.sqrt(width))


def small_kernel(kernel, name, operands, shapes, scratch=()):
    return pl.pallas_call(
        kernel,
        out_shape=[jax.ShapeDtypeStruct(shape, jnp.float32) for shape in shapes],
        in_specs=[pl.BlockSpec(memory_space=pltpu.VMEM)] * len(operands),
        out_specs=[pl.BlockSpec(memory_space=pltpu.VMEM)] * len(shapes),
        scratch_shapes=scratch,
        compiler_params=pltpu.CompilerParams(vmem_limit_bytes=16 << 20),
        name=name,
    )(*operands)


def score_by_rounds(partial, query_grads):
    def heard(code, sources, across):
        got = receive(code.astype(jnp.float16), sources, across)
        swapped = swap(got, "tensor", 1)
        return got.astype(jnp.float32), swapped.astype(jnp.float32)

    seqs, extent = partial.shape
    wide, narrow = (seqs, extent), (seqs, extent - BESIDE)
    other = swap(partial, "tensor", 1)
    mine, code = small_kernel(
        add_cores_kernel, "add_cores", (partial, other), (wide, wide)
    )
    heard_first = heard(code, ROUNDS_OF_8[0][::-1], 1)
    total, code = small_kernel(
        add_first_kernel, "add_first", (mine, *heard_first), (narrow, wide)
    )
    heard_second = heard(code, ROUNDS_OF_8[1], 0)
    return small_kernel(
        score_kernel,
        "score",
        (total, *heard_second, query_grads),
        ((seqs, query_grads.shape[0]),),
        [pltpu.VMEM(narrow, jnp.bfloat16)],
    )[0]


def add_steps(partial):
    half = (partial.shape[1] - BESIDE) // 2
    even = lax.axis_index("tensor") == odd(lax.axis_index("dp"))
    low, high = partial[:, :half], partial[:, half : 2 * half]
    given = jnp.where(even, high, low)
    total = jnp.where(even, low, high) + swap(given, "tensor", 1)
    bits = steps(lax.axis_size("dp"))
    for pair in zip(bits, bits[::-1]):
        total = total + flip(total, pair)
    return ordered(even, total, swap(total, "tensor", 1), 1)


def on_device(layer_input, gate_grad, factor_in, factor_out, precondition, query_grads):
    own_rows, width = precondition.shape
    dp, dp_size = lax.axis_index("dp"), lax.axis_size("dp")

    sides = project(layer_input, gate_grad, factor_in, factor_out)
    other = swap(sides, "tensor", 1)
    gradient = gradient_rows(sides, other, dp_size)

    held = [gradient]
    rounds = gather_rounds(dp_size)
    for number, (sources, swaps) in enumerate(rounds):
        if number == len(rounds) - 1:
            given, kept = pack(held, sources)
            got = receive(given, sources)
            parts = [kept, got] + ([swap(got, "tensor", 1)] if swaps else [])
        else:
            given = held[0] if number == 0 else jnp.stack(held)
            got = receive(given, sources)
            heard = [got] + ([swap(got, "tensor", 1)] if swaps else [])
            held += [row for rows in heard for row in (rows if number else [rows])]
    matrices = split_bands([precondition], got)

    partial = precondition_rows(parts, got, matrices, dp_size)

    if dp_size == 8:
        return score_by_rounds(partial, query_grads)
    rounded = add_steps(partial).astype(jnp.bfloat16)
    return contract_last(rounded, query_grads) * (1 / math.sqrt(width))


def solution(mesh):
    in_specs = (
        P(("groups", "dp"), "tensor"),
        P(("groups", "dp"), "tensor"),
        P(None, "tensor"),
        P(None, "tensor"),
        P(("dp", "tensor"), None),
        P(("dp", "tensor"), None),
    )
    out_specs = P("groups", ("dp", "tensor"))
    return jax.shard_map(
        on_device, mesh=mesh, in_specs=in_specs, out_specs=out_specs, check_vma=False
    )
```

```python
import functools
import math

import jax
import jax.numpy as jnp
from jax import lax
from jax.experimental import pallas as pl
from jax.experimental.pallas import tpu as pltpu
from jax.sharding import PartitionSpec as P

CHUNK = 1024
BAND = 512
BESIDE = 128
LAST = (((1,), (1,)), ((), ()))

ROUNDS_OF_8 = (
    ((2, 3, 0, 1, 6, 7, 4, 5), (4, 5, 1, 0, 7, 6, 2, 3)),
    ((1, 0, 4, 5, 2, 3, 7, 6), (4, 5, 1, 0, 7, 6, 2, 3)),
)


def gather_rounds(size):
    if size == 8:
        return [(pair, True) for pair in ROUNDS_OF_8]
    rounds = []
    for bit in steps(size):
        sources = tuple(i ^ bit for i in range(size))
        rounds.append(((sources, sources), False))
    return rounds


def gather_slots(size):
    held = [[[chip] for chip in range(size)] for _ in range(2)]
    for sources, swaps in gather_rounds(size):
        got = [[held[c][sources[c][i]] for i in range(size)] for c in range(2)]
        held = [
            [
                held[c][i] + got[c][i] + (got[1 - c][i] if swaps else [])
                for i in range(size)
            ]
            for c in range(2)
        ]
    return [[[row.index(s) for s in range(size)] for row in rows] for rows in held]


def packed(values, bits):
    word = sum(value << (bits * i) for i, value in enumerate(values))
    return word - (1 << 32) if word >= 1 << 31 else word


def unpacked(word, index, bits):
    return (word >> (bits * index)) & ((1 << bits) - 1)


def gather_target(sources, core, dp):
    size = len(sources[0])
    if size != 8:
        return dp ^ sources[0][0]
    words = [packed([row.index(i) for i in range(size)], 3) for row in sources]
    return unpacked(jnp.where(core == 0, words[0], words[1]), dp, 3)


def gather_slot(size):
    core, dp = lax.axis_index("tensor"), lax.axis_index("dp")
    if size != 8:
        return lambda s: dp ^ s
    place, word = core * size + dp, jnp.int32(0)
    for k, row in enumerate(sum(gather_slots(size), [])):
        word = jnp.where(place == k, jnp.int32(packed(row, 4)), word)
    return lambda s: unpacked(word, s, 4)


def project_kernel(layer_ref, gate_ref, in_ref, out_ref, sides_ref, left, right, sems):
    rank, tokens = in_ref.shape[0], layer_ref.shape[0]
    counts = (layer_ref.shape[1] // CHUNK, gate_ref.shape[1] // CHUNK)
    copies = []
    for part, (big, small) in enumerate(((layer_ref, in_ref), (gate_ref, out_ref))):
        for c in range(counts[part]):
            slot = len(copies)
            cols = pl.ds(c * CHUNK, CHUNK)
            copies.append(
                (
                    pltpu.make_async_copy(
                        small.at[:, cols],
                        right.at[slot, pl.ds(part * rank, rank)],
                        sems.at[0, slot],
                    ),
                    pltpu.make_async_copy(
                        big.at[:, cols], left.at[slot], sems.at[1, slot]
                    ),
                )
            )
    for pair in copies:
        for copy in pair:
            copy.start()
    blank = jnp.zeros((rank, CHUNK), right.dtype)
    for slot in range(len(copies)):
        right[slot, pl.ds(rank if slot < counts[0] else 0, rank)] = blank
    half = tokens // 2
    totals = [None, None]
    for slot, pair in enumerate(copies):
        for copy in pair:
            copy.wait()
        for h in range(2):
            term = lax.dot_general(
                left[slot, h * half : (h + 1) * half],
                right[slot],
                LAST,
                preferred_element_type=jnp.float32,
            )
            totals[h] = term if slot == 0 else totals[h] + term
    for h in range(2):
        sides_ref[h * half : (h + 1) * half] = totals[h]


def project(layer_input, gate_grad, factor_in, factor_out):
    tokens, rank = layer_input.shape[0], factor_in.shape[0]
    features = layer_input.shape[1] + gate_grad.shape[1]
    slots = features // CHUNK
    return pl.pallas_call(
        project_kernel,
        out_shape=jax.ShapeDtypeStruct((tokens, 2 * rank), jnp.float32),
        in_specs=[pl.BlockSpec(memory_space=pl.ANY)] * 4,
        out_specs=pl.BlockSpec(memory_space=pltpu.VMEM),
        scratch_shapes=[
            pltpu.VMEM((slots, tokens, CHUNK), layer_input.dtype),
            pltpu.VMEM((slots, 2 * rank, CHUNK), factor_in.dtype),
            pltpu.SemaphoreType.DMA((2, slots)),
        ],
        compiler_params=pltpu.CompilerParams(vmem_limit_bytes=54784 << 10),
        cost_estimate=pl.CostEstimate(
            flops=2 * tokens * features * rank,
            bytes_accessed=2 * (tokens + rank) * features,
            transcendentals=0,
        ),
        name="project",
    )(layer_input, gate_grad, factor_in, factor_out)


def gradient_kernel(mine_ref, other_ref, result_ref, square):
    tokens, rank = mine_ref.shape[0], square.shape[0]
    terms = jnp.concatenate(split(mine_ref[...] + other_ref[...]), axis=1)
    terms = terms.astype(jnp.bfloat16)
    product = lax.dot_general(
        terms, terms, (((0,), (0,)), ((), ())), preferred_element_type=jnp.float32
    )

    def block(i, j):
        rows = product[2 * rank * i : 2 * rank * i + rank]
        return rows[:, 2 * rank * j : 2 * rank * (j + 1)]

    full = block(0, 0) + (block(0, 1) + block(1, 0) + block(1, 1))
    square[...] = full[:, rank:] * (1 / math.sqrt(tokens))
    rows = result_ref.shape[0]
    each = rank // rows
    for k in range(each):
        result_ref[:, k * rank : (k + 1) * rank] = square[pl.ds(k, rows, each), :]


def gradient_rows(mine, other, rows):
    tokens, rank = mine.shape[0], mine.shape[1] // 2
    return pl.pallas_call(
        gradient_kernel,
        out_shape=jax.ShapeDtypeStruct((rows, rank * rank // rows), jnp.float32),
        in_specs=[pl.BlockSpec(memory_space=pltpu.VMEM)] * 2,
        out_specs=pl.BlockSpec(memory_space=pltpu.VMEM),
        scratch_shapes=[pltpu.VMEM((rank, rank), jnp.float32)],
        compiler_params=pltpu.CompilerParams(vmem_limit_bytes=16 << 20),
        cost_estimate=pl.CostEstimate(
            flops=2 * tokens * rank * rank,
            bytes_accessed=16 * tokens * rank,
            transcendentals=0,
        ),
        name="gradient",
    )(mine, other)


def split(value):
    high = value.astype(jnp.bfloat16).astype(jnp.float32)
    return high, value - high


def pack_kernel(sources, *refs):
    *held_refs, given_ref, kept_ref = refs
    core, dp = lax.axis_index("tensor"), lax.axis_index("dp")
    target = gather_target(sources, core, dp)
    for row, ref in enumerate(held_refs):
        given_ref[row : row + 1] = ref[pl.ds(target, 1), :]
        kept_ref[row : row + 1] = ref[pl.ds(dp, 1), :]


def pack(held, sources):
    return pl.pallas_call(
        functools.partial(pack_kernel, sources),
        out_shape=[jax.ShapeDtypeStruct((len(held), held[0].shape[1]), jnp.float32)] * 2,
        in_specs=[pl.BlockSpec(memory_space=pltpu.VMEM)] * len(held),
        out_specs=[pl.BlockSpec(memory_space=pltpu.VMEM)] * 2,
        compiler_params=pltpu.CompilerParams(vmem_limit_bytes=16 << 20),
        name="pack",
    )(*held)


def split_kernel(after_ref, *refs):
    del after_ref
    *bands, high_ref, low_ref = refs
    first = 0
    for band_ref in bands:
        for start in range(0, band_ref.shape[1], BAND):
            lanes = slice(first + start, first + start + BAND)
            high, low = split(band_ref[:, start : start + BAND])
            high_ref[:, lanes] = high.astype(jnp.bfloat16)
            low_ref[:, lanes] = low.astype(jnp.bfloat16)
        first += band_ref.shape[1]


def split_bands(bands, after):
    shape = (bands[0].shape[0], sum(band.shape[1] for band in bands))
    return pl.pallas_call(
        split_kernel,
        out_shape=[jax.ShapeDtypeStruct(shape, jnp.bfloat16)] * 2,
        in_specs=[pl.BlockSpec(memory_space=pl.ANY)]
        + [pl.BlockSpec(memory_space=pltpu.VMEM)] * len(bands),
        out_specs=[pl.BlockSpec(memory_space=pltpu.VMEM)] * 2,
        compiler_params=pltpu.CompilerParams(vmem_limit_bytes=16 << 20),
        cost_estimate=pl.CostEstimate(
            flops=0, bytes_accessed=8 * shape[0] * shape[1], transcendentals=0
        ),
        name="split",
    )(after, *bands)


def precondition_kernel(token_ref, *refs):
    del token_ref
    *refs, result_ref, held = refs
    *part_refs, high_ref, low_ref = refs
    seqs, rows = result_ref.shape[0], held.shape[1]
    core, first = lax.axis_index("tensor"), 0
    for part_ref in part_refs:
        own = jnp.where(core == 0, part_ref[:, :rows], part_ref[:, rows:])
        held[first : first + part_ref.shape[0]] = own
        first += part_ref.shape[0]
    slot = gather_slot(seqs)
    grads = jnp.concatenate(
        [held[pl.ds(slot(s), 1), :] for s in range(seqs)], axis=0
    )
    grads = jnp.concatenate(split(grads), axis=0).astype(jnp.bfloat16)
    width = high_ref.shape[1]
    for start in range(0, width, BAND):
        lanes = slice(start, start + BAND)
        by_high, by_low = (
            jnp.dot(grads, ref[:, lanes], preferred_element_type=jnp.float32)
            for ref in (high_ref, low_ref)
        )
        small = by_high[seqs:] + by_low[:seqs] + by_low[seqs:]
        result_ref[:, lanes] = by_high[:seqs] + small
    top = jnp.max(jnp.abs(result_ref[:, :width]), axis=1, keepdims=True)
    power = jnp.floor(jnp.log2(jnp.clip(top, 1e-30, 1e30))) - 14
    result_ref[:, width:] = jnp.broadcast_to(power, (seqs, BESIDE))


def precondition_rows(parts, token, matrices, seqs):
    rows, width = matrices[0].shape
    held = sum(part.shape[0] for part in parts)
    return pl.pallas_call(
        precondition_kernel,
        out_shape=jax.ShapeDtypeStruct((seqs, width + BESIDE), jnp.float32),
        in_specs=[pl.BlockSpec(memory_space=pl.ANY)]
        + [pl.BlockSpec(memory_space=pltpu.VMEM)] * (len(parts) + len(matrices)),
        out_specs=pl.BlockSpec(memory_space=pltpu.VMEM),
        scratch_shapes=[pltpu.VMEM((held, rows), jnp.float32)],
        compiler_params=pltpu.CompilerParams(vmem_limit_bytes=16 << 20),
        cost_estimate=pl.CostEstimate(
            flops=2 * seqs * rows * width,
            bytes_accessed=4 * rows * width,
            transcendentals=0,
        ),
        name="precondition",
    )(token, *parts, *matrices)


def contract_last(left, right):
    return lax.dot_general(left, right, LAST, preferred_element_type=jnp.float32)


def swap(value, axis, bit):
    size = lax.axis_size(axis)
    return lax.ppermute(value, axis, [(i, i ^ bit) for i in range(size)])


def receive(value, sources, across=0):
    pairs = [
        (2 * source + (core ^ across), 2 * chip + core)
        for core in range(2)
        for chip, source in enumerate(sources[core])
    ]
    return lax.ppermute(value, ("dp", "tensor"), pairs)


def flip(value, steps):
    size = lax.axis_size("dp")
    pairs = []
    for place in range(2 * size):
        family = (place ^ odd(place >> 1)) & 1
        pairs.append((place, place ^ (2 * steps[family] + 1)))
    return lax.ppermute(value, ("dp", "tensor"), pairs)


def odd(number):
    for shift in (8, 4, 2, 1):
        number = number ^ (number >> shift)
    return number & 1


def steps(size):
    return [1 << i for i in range(size.bit_length() - 1)]


def ordered(first, mine, other, axis):
    return jnp.where(
        first,
        jnp.concatenate((mine, other), axis),
        jnp.concatenate((other, mine), axis),
    )


def add_cores_kernel(mine_ref, other_ref, sum_ref, code_ref):
    width = sum_ref.shape[1] - BESIDE
    power = jnp.maximum(mine_ref[:, width:], other_ref[:, width:]) + 1
    scale = jnp.exp2(-power)
    for start in range(0, width, BESIDE):
        lanes = slice(start, start + BESIDE)
        total = mine_ref[:, lanes] + other_ref[:, lanes]
        sum_ref[:, lanes] = total
        code_ref[:, lanes] = total * scale
    sum_ref[:, width:] = power
    code_ref[:, width:] = power


def add_first_kernel(mine_ref, got_ref, swapped_ref, sum_ref, code_ref):
    width = sum_ref.shape[1]
    powers = [ref[:, width:] for ref in (mine_ref, got_ref, swapped_ref)]
    power = jnp.maximum(jnp.maximum(powers[0], powers[1]), powers[2]) + 2
    got_scale, swapped_scale = jnp.exp2(powers[1]), jnp.exp2(powers[2])
    scale = jnp.exp2(-power)
    own = jnp.where(lax.axis_index("tensor") == 0, 1.0, 0.0)
    for start in range(0, width, BESIDE):
        lanes = slice(start, start + BESIDE)
        first = got_ref[:, lanes] * got_scale + swapped_ref[:, lanes] * swapped_scale
        mine = mine_ref[:, lanes]
        sum_ref[:, lanes] = mine + first
        code_ref[:, lanes] = (first + mine * own) * scale
    code_ref[:, width:] = power


def score_kernel(sum_ref, got_ref, swapped_ref, query_ref, result_ref, whole):
    width = sum_ref.shape[1]
    got_scale = jnp.exp2(got_ref[:, width:])
    swapped_scale = jnp.exp2(swapped_ref[:, width:])
    for start in range(0, width, BESIDE):
        lanes = slice(start, start + BESIDE)
        second = got_ref[:, lanes] * got_scale + swapped_ref[:, lanes] * swapped_scale
        whole[:, lanes] = sum_ref[:, lanes] + second
    scores = contract_last(whole[...].astype(query_ref.dtype), query_ref[...])
    result_ref[...] = scores * (1 / math.sqrt(width))


def small_kernel(kernel, name, operands, shapes, scratch=()):
    return pl.pallas_call(
        kernel,
        out_shape=[jax.ShapeDtypeStruct(shape, jnp.float32) for shape in shapes],
        in_specs=[pl.BlockSpec(memory_space=pltpu.VMEM)] * len(operands),
        out_specs=[pl.BlockSpec(memory_space=pltpu.VMEM)] * len(shapes),
        scratch_shapes=scratch,
        compiler_params=pltpu.CompilerParams(vmem_limit_bytes=16 << 20),
        name=name,
    )(*operands)


def score_by_rounds(partial, query_grads):
    def heard(code, sources, across):
        got = receive(code.astype(jnp.float16), sources, across)
        swapped = swap(got, "tensor", 1)
        return got.astype(jnp.float32), swapped.astype(jnp.float32)

    seqs, extent = partial.shape
    wide, narrow = (seqs, extent), (seqs, extent - BESIDE)
    other = swap(partial, "tensor", 1)
    mine, code = small_kernel(
        add_cores_kernel, "add_cores", (partial, other), (wide, wide)
    )
    heard_first = heard(code, ROUNDS_OF_8[0][::-1], 1)
    total, code = small_kernel(
        add_first_kernel, "add_first", (mine, *heard_first), (narrow, wide)
    )
    heard_second = heard(code, ROUNDS_OF_8[1], 0)
    return small_kernel(
        score_kernel,
        "score",
        (total, *heard_second, query_grads),
        ((seqs, query_grads.shape[0]),),
        [pltpu.VMEM(narrow, jnp.float32)],
    )[0]


def add_steps(partial):
    half = (partial.shape[1] - BESIDE) // 2
    even = lax.axis_index("tensor") == odd(lax.axis_index("dp"))
    low, high = partial[:, :half], partial[:, half : 2 * half]
    given = jnp.where(even, high, low)
    total = jnp.where(even, low, high) + swap(given, "tensor", 1)
    bits = steps(lax.axis_size("dp"))
    for pair in zip(bits, bits[::-1]):
        total = total + flip(total, pair)
    return ordered(even, total, swap(total, "tensor", 1), 1)


def on_device(layer_input, gate_grad, factor_in, factor_out, precondition, query_grads):
    own_rows, width = precondition.shape
    dp, dp_size = lax.axis_index("dp"), lax.axis_size("dp")

    sides = project(layer_input, gate_grad, factor_in, factor_out)
    other = swap(sides, "tensor", 1)
    gradient = gradient_rows(sides, other, dp_size)

    held = [gradient]
    rounds = gather_rounds(dp_size)
    for number, (sources, swaps) in enumerate(rounds):
        if number == len(rounds) - 1:
            given, kept = pack(held, sources)
            got = receive(given, sources)
            parts = [kept, got] + ([swap(got, "tensor", 1)] if swaps else [])
        else:
            given = held[0] if number == 0 else jnp.stack(held)
            got = receive(given, sources)
            heard = [got] + ([swap(got, "tensor", 1)] if swaps else [])
            held += [row for rows in heard for row in (rows if number else [rows])]
    matrices = split_bands([precondition], got)

    partial = precondition_rows(parts, got, matrices, dp_size)

    if dp_size == 8:
        return score_by_rounds(partial, query_grads)
    rounded = add_steps(partial).astype(jnp.bfloat16)
    return contract_last(rounded, query_grads) * (1 / math.sqrt(width))


def solution(mesh):
    in_specs = (
        P(("groups", "dp"), "tensor"),
        P(("groups", "dp"), "tensor"),
        P(None, "tensor"),
        P(None, "tensor"),
        P(("dp", "tensor"), None),
        P(("dp", "tensor"), None),
    )
    out_specs = P("groups", ("dp", "tensor"))
    return jax.shard_map(
        on_device, mesh=mesh, in_specs=in_specs, out_specs=out_specs, check_vma=False
    )
```

```python
import functools
import math

import jax
import jax.numpy as jnp
from jax import lax
from jax.experimental import pallas as pl
from jax.experimental.pallas import tpu as pltpu
from jax.sharding import PartitionSpec as P

CHUNK = 1024
BAND = 1024
BESIDE = 128
LAST = (((1,), (1,)), ((), ()))

ROUNDS_OF_8 = (
    ((2, 3, 0, 1, 6, 7, 4, 5), (4, 5, 1, 0, 7, 6, 2, 3)),
    ((1, 0, 4, 5, 2, 3, 7, 6), (4, 5, 1, 0, 7, 6, 2, 3)),
)


def gather_rounds(size):
    if size == 8:
        return [(pair, True) for pair in ROUNDS_OF_8]
    rounds = []
    for bit in steps(size):
        sources = tuple(i ^ bit for i in range(size))
        rounds.append(((sources, sources), False))
    return rounds


def gather_slots(size):
    held = [[[chip] for chip in range(size)] for _ in range(2)]
    for sources, swaps in gather_rounds(size):
        got = [[held[c][sources[c][i]] for i in range(size)] for c in range(2)]
        held = [
            [
                held[c][i] + got[c][i] + (got[1 - c][i] if swaps else [])
                for i in range(size)
            ]
            for c in range(2)
        ]
    return [[[row.index(s) for s in range(size)] for row in rows] for rows in held]


def packed(values, bits):
    word = sum(value << (bits * i) for i, value in enumerate(values))
    return word - (1 << 32) if word >= 1 << 31 else word


def unpacked(word, index, bits):
    return (word >> (bits * index)) & ((1 << bits) - 1)


def gather_target(sources, core, dp):
    size = len(sources[0])
    if size != 8:
        return dp ^ sources[0][0]
    words = [packed([row.index(i) for i in range(size)], 3) for row in sources]
    return unpacked(jnp.where(core == 0, words[0], words[1]), dp, 3)


def gather_slot(size):
    core, dp = lax.axis_index("tensor"), lax.axis_index("dp")
    if size != 8:
        return lambda s: dp ^ s
    place, word = core * size + dp, jnp.int32(0)
    for k, row in enumerate(sum(gather_slots(size), [])):
        word = jnp.where(place == k, jnp.int32(packed(row, 4)), word)
    return lambda s: unpacked(word, s, 4)


def project_kernel(layer_ref, gate_ref, in_ref, out_ref, sides_ref, left, right, sems):
    rank, tokens = in_ref.shape[0], layer_ref.shape[0]
    counts = (layer_ref.shape[1] // CHUNK, gate_ref.shape[1] // CHUNK)
    copies = []
    for part, (big, small) in enumerate(((layer_ref, in_ref), (gate_ref, out_ref))):
        for c in range(counts[part]):
            slot = len(copies)
            cols = pl.ds(c * CHUNK, CHUNK)
            copies.append(
                (
                    pltpu.make_async_copy(
                        small.at[:, cols],
                        right.at[slot, pl.ds(part * rank, rank)],
                        sems.at[0, slot],
                    ),
                    pltpu.make_async_copy(
                        big.at[:, cols], left.at[slot], sems.at[1, slot]
                    ),
                )
            )
    for pair in copies:
        for copy in pair:
            copy.start()
    blank = jnp.zeros((rank, CHUNK), right.dtype)
    for slot in range(len(copies)):
        right[slot, pl.ds(rank if slot < counts[0] else 0, rank)] = blank
    half = tokens // 2
    totals = [None, None]
    for slot, pair in enumerate(copies):
        for copy in pair:
            copy.wait()
        for h in range(2):
            term = lax.dot_general(
                left[slot, h * half : (h + 1) * half],
                right[slot],
                LAST,
                preferred_element_type=jnp.float32,
            )
            totals[h] = term if slot == 0 else totals[h] + term
    for h in range(2):
        sides_ref[h * half : (h + 1) * half] = totals[h]


def project(layer_input, gate_grad, factor_in, factor_out):
    tokens, rank = layer_input.shape[0], factor_in.shape[0]
    features = layer_input.shape[1] + gate_grad.shape[1]
    slots = features // CHUNK
    return pl.pallas_call(
        project_kernel,
        out_shape=jax.ShapeDtypeStruct((tokens, 2 * rank), jnp.float32),
        in_specs=[pl.BlockSpec(memory_space=pl.ANY)] * 4,
        out_specs=pl.BlockSpec(memory_space=pltpu.VMEM),
        scratch_shapes=[
            pltpu.VMEM((slots, tokens, CHUNK), layer_input.dtype),
            pltpu.VMEM((slots, 2 * rank, CHUNK), factor_in.dtype),
            pltpu.SemaphoreType.DMA((2, slots)),
        ],
        compiler_params=pltpu.CompilerParams(vmem_limit_bytes=54784 << 10),
        cost_estimate=pl.CostEstimate(
            flops=2 * tokens * features * rank,
            bytes_accessed=2 * (tokens + rank) * features,
            transcendentals=0,
        ),
        name="project",
    )(layer_input, gate_grad, factor_in, factor_out)


def gradient_kernel(mine_ref, other_ref, result_ref, square):
    tokens, rank = mine_ref.shape[0], square.shape[0]
    terms = jnp.concatenate(split(mine_ref[...] + other_ref[...]), axis=1)
    terms = terms.astype(jnp.bfloat16)
    product = lax.dot_general(
        terms, terms, (((0,), (0,)), ((), ())), preferred_element_type=jnp.float32
    )

    def block(i, j):
        rows = product[2 * rank * i : 2 * rank * i + rank]
        return rows[:, 2 * rank * j : 2 * rank * (j + 1)]

    full = block(0, 0) + (block(0, 1) + block(1, 0) + block(1, 1))
    square[...] = full[:, rank:] * (1 / math.sqrt(tokens))
    rows = result_ref.shape[0]
    each = rank // rows
    for k in range(each):
        result_ref[:, k * rank : (k + 1) * rank] = square[pl.ds(k, rows, each), :]


def gradient_rows(mine, other, rows):
    tokens, rank = mine.shape[0], mine.shape[1] // 2
    return pl.pallas_call(
        gradient_kernel,
        out_shape=jax.ShapeDtypeStruct((rows, rank * rank // rows), jnp.float32),
        in_specs=[pl.BlockSpec(memory_space=pltpu.VMEM)] * 2,
        out_specs=pl.BlockSpec(memory_space=pltpu.VMEM),
        scratch_shapes=[pltpu.VMEM((rank, rank), jnp.float32)],
        compiler_params=pltpu.CompilerParams(vmem_limit_bytes=16 << 20),
        cost_estimate=pl.CostEstimate(
            flops=2 * tokens * rank * rank,
            bytes_accessed=16 * tokens * rank,
            transcendentals=0,
        ),
        name="gradient",
    )(mine, other)


def split(value):
    high = value.astype(jnp.bfloat16).astype(jnp.float32)
    return high, value - high


def pack_kernel(sources, *refs):
    *held_refs, given_ref, kept_ref = refs
    core, dp = lax.axis_index("tensor"), lax.axis_index("dp")
    target = gather_target(sources, core, dp)
    for row, ref in enumerate(held_refs):
        given_ref[row : row + 1] = ref[pl.ds(target, 1), :]
        kept_ref[row : row + 1] = ref[pl.ds(dp, 1), :]


def pack(held, sources):
    return pl.pallas_call(
        functools.partial(pack_kernel, sources),
        out_shape=[jax.ShapeDtypeStruct((len(held), held[0].shape[1]), jnp.float32)] * 2,
        in_specs=[pl.BlockSpec(memory_space=pltpu.VMEM)] * len(held),
        out_specs=[pl.BlockSpec(memory_space=pltpu.VMEM)] * 2,
        compiler_params=pltpu.CompilerParams(vmem_limit_bytes=16 << 20),
        name="pack",
    )(*held)


def split_kernel(after_ref, *refs):
    del after_ref
    *bands, high_ref, low_ref = refs
    first = 0
    for band_ref in bands:
        for start in range(0, band_ref.shape[1], BAND):
            lanes = slice(first + start, first + start + BAND)
            high, low = split(band_ref[:, start : start + BAND])
            high_ref[:, lanes] = high.astype(jnp.bfloat16)
            low_ref[:, lanes] = low.astype(jnp.bfloat16)
        first += band_ref.shape[1]


def split_bands(bands, after):
    shape = (bands[0].shape[0], sum(band.shape[1] for band in bands))
    return pl.pallas_call(
        split_kernel,
        out_shape=[jax.ShapeDtypeStruct(shape, jnp.bfloat16)] * 2,
        in_specs=[pl.BlockSpec(memory_space=pl.ANY)]
        + [pl.BlockSpec(memory_space=pltpu.VMEM)] * len(bands),
        out_specs=[pl.BlockSpec(memory_space=pltpu.VMEM)] * 2,
        compiler_params=pltpu.CompilerParams(vmem_limit_bytes=16 << 20),
        cost_estimate=pl.CostEstimate(
            flops=0, bytes_accessed=8 * shape[0] * shape[1], transcendentals=0
        ),
        name="split",
    )(after, *bands)


def precondition_kernel(token_ref, *refs):
    del token_ref
    *refs, result_ref, held = refs
    *part_refs, high_ref, low_ref = refs
    seqs, rows = result_ref.shape[0], held.shape[1]
    core, first = lax.axis_index("tensor"), 0
    for part_ref in part_refs:
        own = jnp.where(core == 0, part_ref[:, :rows], part_ref[:, rows:])
        held[first : first + part_ref.shape[0]] = own
        first += part_ref.shape[0]
    slot = gather_slot(seqs)
    grads = jnp.concatenate(
        [held[pl.ds(slot(s), 1), :] for s in range(seqs)], axis=0
    )
    grads = jnp.concatenate(split(grads), axis=0).astype(jnp.bfloat16)
    width = high_ref.shape[1]
    for start in range(0, width, BAND):
        lanes = slice(start, start + BAND)
        by_high, by_low = (
            jnp.dot(grads, ref[:, lanes], preferred_element_type=jnp.float32)
            for ref in (high_ref, low_ref)
        )
        small = by_high[seqs:] + by_low[:seqs] + by_low[seqs:]
        result_ref[:, lanes] = by_high[:seqs] + small
    top = jnp.max(jnp.abs(result_ref[:, :width]), axis=1, keepdims=True)
    power = jnp.floor(jnp.log2(jnp.clip(top, 1e-30, 1e30))) - 14
    result_ref[:, width:] = jnp.broadcast_to(power, (seqs, BESIDE))


def precondition_rows(parts, token, matrices, seqs):
    rows, width = matrices[0].shape
    held = sum(part.shape[0] for part in parts)
    return pl.pallas_call(
        precondition_kernel,
        out_shape=jax.ShapeDtypeStruct((seqs, width + BESIDE), jnp.float32),
        in_specs=[pl.BlockSpec(memory_space=pl.ANY)]
        + [pl.BlockSpec(memory_space=pltpu.VMEM)] * (len(parts) + len(matrices)),
        out_specs=pl.BlockSpec(memory_space=pltpu.VMEM),
        scratch_shapes=[pltpu.VMEM((held, rows), jnp.float32)],
        compiler_params=pltpu.CompilerParams(vmem_limit_bytes=16 << 20),
        cost_estimate=pl.CostEstimate(
            flops=2 * seqs * rows * width,
            bytes_accessed=4 * rows * width,
            transcendentals=0,
        ),
        name="precondition",
    )(token, *parts, *matrices)


def contract_last(left, right):
    return lax.dot_general(left, right, LAST, preferred_element_type=jnp.float32)


def swap(value, axis, bit):
    size = lax.axis_size(axis)
    return lax.ppermute(value, axis, [(i, i ^ bit) for i in range(size)])


def receive(value, sources, across=0):
    pairs = [
        (2 * source + (core ^ across), 2 * chip + core)
        for core in range(2)
        for chip, source in enumerate(sources[core])
    ]
    return lax.ppermute(value, ("dp", "tensor"), pairs)


def flip(value, steps):
    size = lax.axis_size("dp")
    pairs = []
    for place in range(2 * size):
        family = (place ^ odd(place >> 1)) & 1
        pairs.append((place, place ^ (2 * steps[family] + 1)))
    return lax.ppermute(value, ("dp", "tensor"), pairs)


def odd(number):
    for shift in (8, 4, 2, 1):
        number = number ^ (number >> shift)
    return number & 1


def steps(size):
    return [1 << i for i in range(size.bit_length() - 1)]


def ordered(first, mine, other, axis):
    return jnp.where(
        first,
        jnp.concatenate((mine, other), axis),
        jnp.concatenate((other, mine), axis),
    )


def add_cores_kernel(mine_ref, other_ref, sum_ref, code_ref):
    width = sum_ref.shape[1] - BESIDE
    power = jnp.maximum(mine_ref[:, width:], other_ref[:, width:]) + 1
    scale = jnp.exp2(-power)
    for start in range(0, width, BESIDE):
        lanes = slice(start, start + BESIDE)
        total = mine_ref[:, lanes] + other_ref[:, lanes]
        sum_ref[:, lanes] = total
        code_ref[:, lanes] = total * scale
    sum_ref[:, width:] = power
    code_ref[:, width:] = power


def add_first_kernel(mine_ref, got_ref, swapped_ref, sum_ref, code_ref):
    width = sum_ref.shape[1]
    powers = [ref[:, width:] for ref in (mine_ref, got_ref, swapped_ref)]
    power = jnp.maximum(jnp.maximum(powers[0], powers[1]), powers[2]) + 2
    got_scale, swapped_scale = jnp.exp2(powers[1]), jnp.exp2(powers[2])
    scale = jnp.exp2(-power)
    own = jnp.where(lax.axis_index("tensor") == 0, 1.0, 0.0)
    for start in range(0, width, BESIDE):
        lanes = slice(start, start + BESIDE)
        first = got_ref[:, lanes] * got_scale + swapped_ref[:, lanes] * swapped_scale
        mine = mine_ref[:, lanes]
        sum_ref[:, lanes] = mine + first
        code_ref[:, lanes] = (first + mine * own) * scale
    code_ref[:, width:] = power


def score_kernel(sum_ref, got_ref, swapped_ref, query_ref, result_ref, whole):
    width = sum_ref.shape[1]
    got_scale = jnp.exp2(got_ref[:, width:])
    swapped_scale = jnp.exp2(swapped_ref[:, width:])
    for start in range(0, width, BESIDE):
        lanes = slice(start, start + BESIDE)
        second = got_ref[:, lanes] * got_scale + swapped_ref[:, lanes] * swapped_scale
        whole[:, lanes] = sum_ref[:, lanes] + second
    scores = contract_last(whole[...].astype(query_ref.dtype), query_ref[...])
    result_ref[...] = scores * (1 / math.sqrt(width))


def small_kernel(kernel, name, operands, shapes, scratch=()):
    return pl.pallas_call(
        kernel,
        out_shape=[jax.ShapeDtypeStruct(shape, jnp.float32) for shape in shapes],
        in_specs=[pl.BlockSpec(memory_space=pltpu.VMEM)] * len(operands),
        out_specs=[pl.BlockSpec(memory_space=pltpu.VMEM)] * len(shapes),
        scratch_shapes=scratch,
        compiler_params=pltpu.CompilerParams(vmem_limit_bytes=16 << 20),
        name=name,
    )(*operands)


def score_by_rounds(partial, query_grads):
    def heard(code, sources, across):
        got = receive(code.astype(jnp.float16), sources, across)
        swapped = swap(got, "tensor", 1)
        return got.astype(jnp.float32), swapped.astype(jnp.float32)

    seqs, extent = partial.shape
    wide, narrow = (seqs, extent), (seqs, extent - BESIDE)
    other = swap(partial, "tensor", 1)
    mine, code = small_kernel(
        add_cores_kernel, "add_cores", (partial, other), (wide, wide)
    )
    heard_first = heard(code, ROUNDS_OF_8[0][::-1], 1)
    total, code = small_kernel(
        add_first_kernel, "add_first", (mine, *heard_first), (narrow, wide)
    )
    heard_second = heard(code, ROUNDS_OF_8[1], 0)
    return small_kernel(
        score_kernel,
        "score",
        (total, *heard_second, query_grads),
        ((seqs, query_grads.shape[0]),),
        [pltpu.VMEM(narrow, jnp.float32)],
    )[0]


def add_steps(partial):
    half = (partial.shape[1] - BESIDE) // 2
    even = lax.axis_index("tensor") == odd(lax.axis_index("dp"))
    low, high = partial[:, :half], partial[:, half : 2 * half]
    given = jnp.where(even, high, low)
    total = jnp.where(even, low, high) + swap(given, "tensor", 1)
    bits = steps(lax.axis_size("dp"))
    for pair in zip(bits, bits[::-1]):
        total = total + flip(total, pair)
    return ordered(even, total, swap(total, "tensor", 1), 1)


def on_device(layer_input, gate_grad, factor_in, factor_out, precondition, query_grads):
    own_rows, width = precondition.shape
    dp, dp_size = lax.axis_index("dp"), lax.axis_size("dp")

    sides = project(layer_input, gate_grad, factor_in, factor_out)
    other = swap(sides, "tensor", 1)
    gradient = gradient_rows(sides, other, dp_size)

    held = [gradient]
    rounds = gather_rounds(dp_size)
    for number, (sources, swaps) in enumerate(rounds):
        if number == len(rounds) - 1:
            given, kept = pack(held, sources)
            got = receive(given, sources)
            parts = [kept, got] + ([swap(got, "tensor", 1)] if swaps else [])
        else:
            given = held[0] if number == 0 else jnp.stack(held)
            got = receive(given, sources)
            heard = [got] + ([swap(got, "tensor", 1)] if swaps else [])
            held += [row for rows in heard for row in (rows if number else [rows])]
    rows, _ = lax.optimization_barrier((precondition, sides))
    matrices = split_bands([rows], got)

    partial = precondition_rows(parts, got, matrices, dp_size)

    if dp_size == 8:
        return score_by_rounds(partial, query_grads)
    rounded = add_steps(partial).astype(jnp.bfloat16)
    return contract_last(rounded, query_grads) * (1 / math.sqrt(width))


def solution(mesh):
    in_specs = (
        P(("groups", "dp"), "tensor"),
        P(("groups", "dp"), "tensor"),
        P(None, "tensor"),
        P(None, "tensor"),
        P(("dp", "tensor"), None),
        P(("dp", "tensor"), None),
    )
    out_specs = P("groups", ("dp", "tensor"))
    return jax.shard_map(
        on_device, mesh=mesh, in_specs=in_specs, out_specs=out_specs, check_vma=False
    )
```

```python
import functools
import math

import jax
import jax.numpy as jnp
from jax import lax
from jax.experimental import pallas as pl
from jax.experimental.pallas import tpu as pltpu
from jax.sharding import PartitionSpec as P

CHUNK = 1024
BAND = 1024
BESIDE = 128
LAST = (((1,), (1,)), ((), ()))

ROUNDS_OF_8 = (
    ((2, 3, 0, 1, 6, 7, 4, 5), (4, 5, 1, 0, 7, 6, 2, 3)),
    ((1, 0, 4, 5, 2, 3, 7, 6), (4, 5, 1, 0, 7, 6, 2, 3)),
)


def gather_rounds(size):
    if size == 8:
        return [(pair, True) for pair in ROUNDS_OF_8]
    rounds = []
    for bit in steps(size):
        sources = tuple(i ^ bit for i in range(size))
        rounds.append(((sources, sources), False))
    return rounds


def gather_slots(size):
    held = [[[chip] for chip in range(size)] for _ in range(2)]
    for sources, swaps in gather_rounds(size):
        got = [[held[c][sources[c][i]] for i in range(size)] for c in range(2)]
        held = [
            [
                held[c][i] + got[c][i] + (got[1 - c][i] if swaps else [])
                for i in range(size)
            ]
            for c in range(2)
        ]
    return [[[row.index(s) for s in range(size)] for row in rows] for rows in held]


def packed(values, bits):
    word = sum(value << (bits * i) for i, value in enumerate(values))
    return word - (1 << 32) if word >= 1 << 31 else word


def unpacked(word, index, bits):
    return (word >> (bits * index)) & ((1 << bits) - 1)


def gather_target(sources, core, dp):
    size = len(sources[0])
    if size != 8:
        return dp ^ sources[0][0]
    words = [packed([row.index(i) for i in range(size)], 3) for row in sources]
    return unpacked(jnp.where(core == 0, words[0], words[1]), dp, 3)


def first_targets(core, dp):
    first, second = ROUNDS_OF_8
    lists = []
    for row in first:
        targets = [row.index(i) for i in range(8)]
        lists.append([targets] + [[s.index(i) for i in targets] for s in second])
    return [
        unpacked(jnp.where(core == 0, packed(own, 3), packed(other, 3)), dp, 3)
        for own, other in zip(*lists)
    ]


def gather_slot(size):
    core, dp = lax.axis_index("tensor"), lax.axis_index("dp")
    if size != 8:
        return lambda s: dp ^ s
    place, word = core * size + dp, jnp.int32(0)
    for k, row in enumerate(sum(gather_slots(size), [])):
        word = jnp.where(place == k, jnp.int32(packed(row, 4)), word)
    return lambda s: unpacked(word, s, 4)


def project_kernel(layer_ref, gate_ref, in_ref, out_ref, sides_ref, left, right, sems):
    rank, tokens = in_ref.shape[0], layer_ref.shape[0]
    counts = (layer_ref.shape[1] // CHUNK, gate_ref.shape[1] // CHUNK)
    copies = []
    for part, (big, small) in enumerate(((layer_ref, in_ref), (gate_ref, out_ref))):
        for c in range(counts[part]):
            slot = len(copies)
            cols = pl.ds(c * CHUNK, CHUNK)
            copies.append(
                (
                    pltpu.make_async_copy(
                        small.at[:, cols],
                        right.at[slot, pl.ds(part * rank, rank)],
                        sems.at[0, slot],
                    ),
                    pltpu.make_async_copy(
                        big.at[:, cols], left.at[slot], sems.at[1, slot]
                    ),
                )
            )
    for pair in copies:
        for copy in pair:
            copy.start()
    blank = jnp.zeros((rank, CHUNK), right.dtype)
    for slot in range(len(copies)):
        right[slot, pl.ds(rank if slot < counts[0] else 0, rank)] = blank
    half = tokens // 2
    totals = [None, None]
    for slot, pair in enumerate(copies):
        for copy in pair:
            copy.wait()
        for h in range(2):
            term = lax.dot_general(
                left[slot, h * half : (h + 1) * half],
                right[slot],
                LAST,
                preferred_element_type=jnp.float32,
            )
            totals[h] = term if slot == 0 else totals[h] + term
    for h in range(2):
        sides_ref[h * half : (h + 1) * half] = totals[h]


def project(layer_input, gate_grad, factor_in, factor_out):
    tokens, rank = layer_input.shape[0], factor_in.shape[0]
    features = layer_input.shape[1] + gate_grad.shape[1]
    slots = features // CHUNK
    return pl.pallas_call(
        project_kernel,
        out_shape=jax.ShapeDtypeStruct((tokens, 2 * rank), jnp.float32),
        in_specs=[pl.BlockSpec(memory_space=pl.ANY)] * 4,
        out_specs=pl.BlockSpec(memory_space=pltpu.VMEM),
        scratch_shapes=[
            pltpu.VMEM((slots, tokens, CHUNK), layer_input.dtype),
            pltpu.VMEM((slots, 2 * rank, CHUNK), factor_in.dtype),
            pltpu.SemaphoreType.DMA((2, slots)),
        ],
        compiler_params=pltpu.CompilerParams(vmem_limit_bytes=54784 << 10),
        cost_estimate=pl.CostEstimate(
            flops=2 * tokens * features * rank,
            bytes_accessed=2 * (tokens + rank) * features,
            transcendentals=0,
        ),
        name="project",
    )(layer_input, gate_grad, factor_in, factor_out)


def gradient_kernel(mine_ref, other_ref, result_ref, *refs):
    *given_refs, square = refs
    tokens, rank = mine_ref.shape[0], square.shape[0]
    terms = jnp.concatenate(split(mine_ref[...] + other_ref[...]), axis=1)
    terms = terms.astype(jnp.bfloat16)
    product = lax.dot_general(
        terms, terms, (((0,), (0,)), ((), ())), preferred_element_type=jnp.float32
    )

    def block(i, j):
        rows = product[2 * rank * i : 2 * rank * i + rank]
        return rows[:, 2 * rank * j : 2 * rank * (j + 1)]

    full = block(0, 0) + (block(0, 1) + block(1, 0) + block(1, 1))
    square[...] = full[:, rank:] * (1 / math.sqrt(tokens))
    rows = result_ref.shape[0]
    each = rank // rows
    for k in range(each):
        result_ref[:, k * rank : (k + 1) * rank] = square[pl.ds(k, rows, each), :]
    for given_ref in given_refs:
        chips = first_targets(lax.axis_index("tensor"), lax.axis_index("dp"))
        for row, chip in enumerate(chips):
            given_ref[row : row + 1] = result_ref[pl.ds(chip, 1), :]


def gradient_rows(mine, other, rows):
    tokens, rank = mine.shape[0], mine.shape[1] // 2
    counts = (rows, 3) if rows == 8 else (rows,)
    return pl.pallas_call(
        gradient_kernel,
        out_shape=[
            jax.ShapeDtypeStruct((count, rank * rank // rows), jnp.float32)
            for count in counts
        ],
        in_specs=[pl.BlockSpec(memory_space=pltpu.VMEM)] * 2,
        out_specs=[pl.BlockSpec(memory_space=pltpu.VMEM)] * len(counts),
        scratch_shapes=[pltpu.VMEM((rank, rank), jnp.float32)],
        compiler_params=pltpu.CompilerParams(vmem_limit_bytes=16 << 20),
        cost_estimate=pl.CostEstimate(
            flops=2 * tokens * rank * rank,
            bytes_accessed=16 * tokens * rank,
            transcendentals=0,
        ),
        name="gradient",
    )(mine, other)


def split(value):
    high = value.astype(jnp.bfloat16).astype(jnp.float32)
    return high, value - high


def pack_kernel(sources, *refs):
    *held_refs, given_ref, kept_ref = refs
    core, dp = lax.axis_index("tensor"), lax.axis_index("dp")
    target = gather_target(sources, core, dp)
    for row, ref in enumerate(held_refs):
        some = ref.shape[0] < len(sources[0])
        given_ref[row : row + 1] = ref[pl.ds(1 + core if some else target, 1), :]
        kept_ref[row : row + 1] = ref[pl.ds(0 if some else dp, 1), :]


def pack(held, sources):
    return pl.pallas_call(
        functools.partial(pack_kernel, sources),
        out_shape=[jax.ShapeDtypeStruct((len(held), held[0].shape[1]), jnp.float32)] * 2,
        in_specs=[pl.BlockSpec(memory_space=pltpu.VMEM)] * len(held),
        out_specs=[pl.BlockSpec(memory_space=pltpu.VMEM)] * 2,
        compiler_params=pltpu.CompilerParams(vmem_limit_bytes=16 << 20),
        name="pack",
    )(*held)


def split_kernel(after_ref, *refs):
    del after_ref
    *bands, high_ref, low_ref = refs
    first = 0
    for band_ref in bands:
        for start in range(0, band_ref.shape[1], BAND):
            lanes = slice(first + start, first + start + BAND)
            high, low = split(band_ref[:, start : start + BAND])
            high_ref[:, lanes] = high.astype(jnp.bfloat16)
            low_ref[:, lanes] = low.astype(jnp.bfloat16)
        first += band_ref.shape[1]


def split_bands(bands, after):
    shape = (bands[0].shape[0], sum(band.shape[1] for band in bands))
    return pl.pallas_call(
        split_kernel,
        out_shape=[jax.ShapeDtypeStruct(shape, jnp.bfloat16)] * 2,
        in_specs=[pl.BlockSpec(memory_space=pl.ANY)]
        + [pl.BlockSpec(memory_space=pltpu.VMEM)] * len(bands),
        out_specs=[pl.BlockSpec(memory_space=pltpu.VMEM)] * 2,
        compiler_params=pltpu.CompilerParams(vmem_limit_bytes=16 << 20),
        cost_estimate=pl.CostEstimate(
            flops=0, bytes_accessed=8 * shape[0] * shape[1], transcendentals=0
        ),
        name="split",
    )(after, *bands)


def precondition_kernel(token_ref, *refs):
    del token_ref
    *refs, result_ref, held = refs
    *part_refs, high_ref, low_ref = refs
    seqs, rows = result_ref.shape[0], held.shape[1]
    core, first = lax.axis_index("tensor"), 0
    for part_ref in part_refs:
        own = jnp.where(core == 0, part_ref[:, :rows], part_ref[:, rows:])
        held[first : first + part_ref.shape[0]] = own
        first += part_ref.shape[0]
    slot = gather_slot(seqs)
    grads = jnp.concatenate(
        [held[pl.ds(slot(s), 1), :] for s in range(seqs)], axis=0
    )
    grads = jnp.concatenate(split(grads), axis=0).astype(jnp.bfloat16)
    width = high_ref.shape[1]
    for start in range(0, width, BAND):
        lanes = slice(start, start + BAND)
        by_high, by_low = (
            jnp.dot(grads, ref[:, lanes], preferred_element_type=jnp.float32)
            for ref in (high_ref, low_ref)
        )
        small = by_high[seqs:] + by_low[:seqs] + by_low[seqs:]
        result_ref[:, lanes] = by_high[:seqs] + small
    top = jnp.max(jnp.abs(result_ref[:, :width]), axis=1, keepdims=True)
    power = jnp.floor(jnp.log2(jnp.clip(top, 1e-30, 1e30))) - 14
    result_ref[:, width:] = jnp.broadcast_to(power, (seqs, BESIDE))


def precondition_rows(parts, token, matrices, seqs):
    rows, width = matrices[0].shape
    held = sum(part.shape[0] for part in parts)
    return pl.pallas_call(
        precondition_kernel,
        out_shape=jax.ShapeDtypeStruct((seqs, width + BESIDE), jnp.float32),
        in_specs=[pl.BlockSpec(memory_space=pl.ANY)]
        + [pl.BlockSpec(memory_space=pltpu.VMEM)] * (len(parts) + len(matrices)),
        out_specs=pl.BlockSpec(memory_space=pltpu.VMEM),
        scratch_shapes=[pltpu.VMEM((held, rows), jnp.float32)],
        compiler_params=pltpu.CompilerParams(vmem_limit_bytes=16 << 20),
        cost_estimate=pl.CostEstimate(
            flops=2 * seqs * rows * width,
            bytes_accessed=4 * rows * width,
            transcendentals=0,
        ),
        name="precondition",
    )(token, *parts, *matrices)


def contract_last(left, right):
    return lax.dot_general(left, right, LAST, preferred_element_type=jnp.float32)


def swap(value, axis, bit):
    size = lax.axis_size(axis)
    return lax.ppermute(value, axis, [(i, i ^ bit) for i in range(size)])


def receive(value, sources, across=0):
    pairs = [
        (2 * source + (core ^ across), 2 * chip + core)
        for core in range(2)
        for chip, source in enumerate(sources[core])
    ]
    return lax.ppermute(value, ("dp", "tensor"), pairs)


def flip(value, steps):
    size = lax.axis_size("dp")
    pairs = []
    for place in range(2 * size):
        family = (place ^ odd(place >> 1)) & 1
        pairs.append((place, place ^ (2 * steps[family] + 1)))
    return lax.ppermute(value, ("dp", "tensor"), pairs)


def odd(number):
    for shift in (8, 4, 2, 1):
        number = number ^ (number >> shift)
    return number & 1


def steps(size):
    return [1 << i for i in range(size.bit_length() - 1)]


def ordered(first, mine, other, axis):
    return jnp.where(
        first,
        jnp.concatenate((mine, other), axis),
        jnp.concatenate((other, mine), axis),
    )


def add_cores_kernel(mine_ref, other_ref, sum_ref, code_ref):
    width = sum_ref.shape[1] - BESIDE
    power = jnp.maximum(mine_ref[:, width:], other_ref[:, width:]) + 1
    scale = jnp.exp2(-power)
    for start in range(0, width, BESIDE):
        lanes = slice(start, start + BESIDE)
        total = mine_ref[:, lanes] + other_ref[:, lanes]
        sum_ref[:, lanes] = total
        code_ref[:, lanes] = total * scale
    sum_ref[:, width:] = power
    code_ref[:, width:] = power


def add_first_kernel(mine_ref, got_ref, swapped_ref, sum_ref, code_ref):
    width = sum_ref.shape[1]
    powers = [ref[:, width:] for ref in (mine_ref, got_ref, swapped_ref)]
    power = jnp.maximum(jnp.maximum(powers[0], powers[1]), powers[2]) + 2
    got_scale, swapped_scale = jnp.exp2(powers[1]), jnp.exp2(powers[2])
    scale = jnp.exp2(-power)
    own = jnp.where(lax.axis_index("tensor") == 0, 1.0, 0.0)
    for start in range(0, width, BESIDE):
        lanes = slice(start, start + BESIDE)
        first = got_ref[:, lanes] * got_scale + swapped_ref[:, lanes] * swapped_scale
        mine = mine_ref[:, lanes]
        sum_ref[:, lanes] = mine + first
        code_ref[:, lanes] = (first + mine * own) * scale
    code_ref[:, width:] = power


def score_kernel(sum_ref, got_ref, swapped_ref, query_ref, result_ref, whole):
    width = sum_ref.shape[1]
    got_scale = jnp.exp2(got_ref[:, width:])
    swapped_scale = jnp.exp2(swapped_ref[:, width:])
    for start in range(0, width, BESIDE):
        lanes = slice(start, start + BESIDE)
        second = got_ref[:, lanes] * got_scale + swapped_ref[:, lanes] * swapped_scale
        whole[:, lanes] = sum_ref[:, lanes] + second
    scores = contract_last(whole[...].astype(query_ref.dtype), query_ref[...])
    result_ref[...] = scores * (1 / math.sqrt(width))


def small_kernel(kernel, name, operands, shapes, scratch=()):
    return pl.pallas_call(
        kernel,
        out_shape=[jax.ShapeDtypeStruct(shape, jnp.float32) for shape in shapes],
        in_specs=[pl.BlockSpec(memory_space=pltpu.VMEM)] * len(operands),
        out_specs=[pl.BlockSpec(memory_space=pltpu.VMEM)] * len(shapes),
        scratch_shapes=scratch,
        compiler_params=pltpu.CompilerParams(vmem_limit_bytes=16 << 20),
        name=name,
    )(*operands)


def score_by_rounds(partial, query_grads):
    def heard(code, sources, across):
        got = receive(code.astype(jnp.float16), sources, across)
        swapped = swap(got, "tensor", 1)
        return got.astype(jnp.float32), swapped.astype(jnp.float32)

    seqs, extent = partial.shape
    wide, narrow = (seqs, extent), (seqs, extent - BESIDE)
    other = swap(partial, "tensor", 1)
    mine, code = small_kernel(
        add_cores_kernel, "add_cores", (partial, other), (wide, wide)
    )
    heard_first = heard(code, ROUNDS_OF_8[0][::-1], 1)
    total, code = small_kernel(
        add_first_kernel, "add_first", (mine, *heard_first), (narrow, wide)
    )
    heard_second = heard(code, ROUNDS_OF_8[1], 0)
    return small_kernel(
        score_kernel,
        "score",
        (total, *heard_second, query_grads),
        ((seqs, query_grads.shape[0]),),
        [pltpu.VMEM(narrow, jnp.float32)],
    )[0]


def add_steps(partial):
    half = (partial.shape[1] - BESIDE) // 2
    even = lax.axis_index("tensor") == odd(lax.axis_index("dp"))
    low, high = partial[:, :half], partial[:, half : 2 * half]
    given = jnp.where(even, high, low)
    total = jnp.where(even, low, high) + swap(given, "tensor", 1)
    bits = steps(lax.axis_size("dp"))
    for pair in zip(bits, bits[::-1]):
        total = total + flip(total, pair)
    return ordered(even, total, swap(total, "tensor", 1), 1)


def on_device(layer_input, gate_grad, factor_in, factor_out, precondition, query_grads):
    own_rows, width = precondition.shape
    dp, dp_size = lax.axis_index("dp"), lax.axis_size("dp")

    sides = project(layer_input, gate_grad, factor_in, factor_out)
    other = swap(sides, "tensor", 1)
    gradient, *firsts = gradient_rows(sides, other, dp_size)

    held = [gradient]
    rounds = gather_rounds(dp_size)
    for number, (sources, swaps) in enumerate(rounds):
        if number == len(rounds) - 1:
            given, kept = pack(held, sources)
            got = receive(given, sources)
            parts = [kept, got] + ([swap(got, "tensor", 1)] if swaps else [])
        else:
            given = (*firsts, *held)[0] if number == 0 else jnp.stack(held)
            got = receive(given, sources)
            heard = [got] + ([swap(got, "tensor", 1)] if swaps else [])
            held += [row for rows in heard for row in (rows if number else [rows])]
    rows, _ = lax.optimization_barrier((precondition, sides))
    matrices = split_bands([rows], got)

    partial = precondition_rows(parts, got, matrices, dp_size)

    if dp_size == 8:
        return score_by_rounds(partial, query_grads)
    rounded = add_steps(partial).astype(jnp.bfloat16)
    return contract_last(rounded, query_grads) * (1 / math.sqrt(width))


def solution(mesh):
    in_specs = (
        P(("groups", "dp"), "tensor"),
        P(("groups", "dp"), "tensor"),
        P(None, "tensor"),
        P(None, "tensor"),
        P(("dp", "tensor"), None),
        P(("dp", "tensor"), None),
    )
    out_specs = P("groups", ("dp", "tensor"))
    return jax.shard_map(
        on_device, mesh=mesh, in_specs=in_specs, out_specs=out_specs, check_vma=False
    )
```

```python
import functools
import math

import jax
import jax.numpy as jnp
from jax import lax
from jax.experimental import pallas as pl
from jax.experimental.pallas import tpu as pltpu
from jax.sharding import PartitionSpec as P

CHUNK = 1024
BAND = 1024
BESIDE = 128
LAST = (((1,), (1,)), ((), ()))

ROUNDS_OF_8 = (
    ((2, 3, 0, 1, 6, 7, 4, 5), (4, 5, 1, 0, 7, 6, 2, 3)),
    ((1, 0, 4, 5, 2, 3, 7, 6), (4, 5, 1, 0, 7, 6, 2, 3)),
)


def gather_rounds(size):
    if size == 8:
        return [(pair, True) for pair in ROUNDS_OF_8]
    rounds = []
    for bit in steps(size):
        sources = tuple(i ^ bit for i in range(size))
        rounds.append(((sources, sources), False))
    return rounds


def gather_slots(size):
    held = [[[chip] for chip in range(size)] for _ in range(2)]
    for sources, swaps in gather_rounds(size):
        got = [[held[c][sources[c][i]] for i in range(size)] for c in range(2)]
        held = [
            [
                held[c][i] + got[c][i] + (got[1 - c][i] if swaps else [])
                for i in range(size)
            ]
            for c in range(2)
        ]
    return [[[row.index(s) for s in range(size)] for row in rows] for rows in held]


def packed(values, bits):
    word = sum(value << (bits * i) for i, value in enumerate(values))
    return word - (1 << 32) if word >= 1 << 31 else word


def unpacked(word, index, bits):
    return (word >> (bits * index)) & ((1 << bits) - 1)


def gather_target(sources, core, dp):
    size = len(sources[0])
    if size != 8:
        return dp ^ sources[0][0]
    words = [packed([row.index(i) for i in range(size)], 3) for row in sources]
    return unpacked(jnp.where(core == 0, words[0], words[1]), dp, 3)


def first_targets(core, dp):
    first, second = ROUNDS_OF_8
    lists = []
    for row in first:
        targets = [row.index(i) for i in range(8)]
        lists.append([targets] + [[s.index(i) for i in targets] for s in second])
    return [
        unpacked(jnp.where(core == 0, packed(own, 3), packed(other, 3)), dp, 3)
        for own, other in zip(*lists)
    ]


def gather_slot(size):
    core, dp = lax.axis_index("tensor"), lax.axis_index("dp")
    if size != 8:
        return lambda s: dp ^ s
    place, word = core * size + dp, jnp.int32(0)
    for k, row in enumerate(sum(gather_slots(size), [])):
        word = jnp.where(place == k, jnp.int32(packed(row, 4)), word)
    return lambda s: unpacked(word, s, 4)


def project_kernel(layer_ref, gate_ref, in_ref, out_ref, sides_ref, left, right, sems):
    rank, tokens = in_ref.shape[0], layer_ref.shape[0]
    counts = (layer_ref.shape[1] // CHUNK, gate_ref.shape[1] // CHUNK)
    copies = []
    for part, (big, small) in enumerate(((layer_ref, in_ref), (gate_ref, out_ref))):
        for c in range(counts[part]):
            slot = len(copies)
            cols = pl.ds(c * CHUNK, CHUNK)
            copies.append(
                (
                    pltpu.make_async_copy(
                        small.at[:, cols],
                        right.at[slot, pl.ds(part * rank, rank)],
                        sems.at[0, slot],
                    ),
                    pltpu.make_async_copy(
                        big.at[:, cols], left.at[slot], sems.at[1, slot]
                    ),
                )
            )
    for pair in copies:
        for copy in pair:
            copy.start()
    blank = jnp.zeros((rank, CHUNK), right.dtype)
    for slot in range(len(copies)):
        right[slot, pl.ds(rank if slot < counts[0] else 0, rank)] = blank
    half = tokens // 2
    totals = [None, None]
    for slot, pair in enumerate(copies):
        for copy in pair:
            copy.wait()
        for h in range(2):
            term = lax.dot_general(
                left[slot, h * half : (h + 1) * half],
                right[slot],
                LAST,
                preferred_element_type=jnp.float32,
            )
            totals[h] = term if slot == 0 else totals[h] + term
    for h in range(2):
        sides_ref[h * half : (h + 1) * half] = totals[h]


def project(layer_input, gate_grad, factor_in, factor_out):
    tokens, rank = layer_input.shape[0], factor_in.shape[0]
    features = layer_input.shape[1] + gate_grad.shape[1]
    slots = features // CHUNK
    return pl.pallas_call(
        project_kernel,
        out_shape=jax.ShapeDtypeStruct((tokens, 2 * rank), jnp.float32),
        in_specs=[pl.BlockSpec(memory_space=pl.ANY)] * 4,
        out_specs=pl.BlockSpec(memory_space=pltpu.VMEM),
        scratch_shapes=[
            pltpu.VMEM((slots, tokens, CHUNK), layer_input.dtype),
            pltpu.VMEM((slots, 2 * rank, CHUNK), factor_in.dtype),
            pltpu.SemaphoreType.DMA((2, slots)),
        ],
        compiler_params=pltpu.CompilerParams(vmem_limit_bytes=54784 << 10),
        cost_estimate=pl.CostEstimate(
            flops=2 * tokens * features * rank,
            bytes_accessed=2 * (tokens + rank) * features,
            transcendentals=0,
        ),
        name="project",
    )(layer_input, gate_grad, factor_in, factor_out)


def gradient_kernel(mine_ref, other_ref, result_ref, *refs):
    *given_refs, square = refs
    tokens, rank = mine_ref.shape[0], square.shape[0]
    terms = jnp.concatenate(split(mine_ref[...] + other_ref[...]), axis=1)
    terms = terms.astype(jnp.bfloat16)
    product = lax.dot_general(
        terms, terms, (((0,), (0,)), ((), ())), preferred_element_type=jnp.float32
    )

    def block(i, j):
        rows = product[2 * rank * i : 2 * rank * i + rank]
        return rows[:, 2 * rank * j : 2 * rank * (j + 1)]

    full = block(0, 0) + (block(0, 1) + block(1, 0) + block(1, 1))
    square[...] = full[:, rank:] * (1 / math.sqrt(tokens))
    rows = result_ref.shape[0]
    each = rank // rows
    for k in range(each):
        result_ref[:, k * rank : (k + 1) * rank] = square[pl.ds(k, rows, each), :]
    for given_ref in given_refs:
        chips = first_targets(lax.axis_index("tensor"), lax.axis_index("dp"))
        for row, chip in enumerate(chips):
            given_ref[row : row + 1] = result_ref[pl.ds(chip, 1), :]


def gradient_rows(mine, other, rows):
    tokens, rank = mine.shape[0], mine.shape[1] // 2
    counts = (rows, 3) if rows == 8 else (rows,)
    return pl.pallas_call(
        gradient_kernel,
        out_shape=[
            jax.ShapeDtypeStruct((count, rank * rank // rows), jnp.float32)
            for count in counts
        ],
        in_specs=[pl.BlockSpec(memory_space=pltpu.VMEM)] * 2,
        out_specs=[pl.BlockSpec(memory_space=pltpu.VMEM)] * len(counts),
        scratch_shapes=[pltpu.VMEM((rank, rank), jnp.float32)],
        compiler_params=pltpu.CompilerParams(vmem_limit_bytes=16 << 20),
        cost_estimate=pl.CostEstimate(
            flops=2 * tokens * rank * rank,
            bytes_accessed=16 * tokens * rank,
            transcendentals=0,
        ),
        name="gradient",
    )(mine, other)


def split(value):
    high = value.astype(jnp.bfloat16).astype(jnp.float32)
    return high, value - high


def pack_kernel(sources, *refs):
    *held_refs, given_ref, kept_ref = refs
    core, dp = lax.axis_index("tensor"), lax.axis_index("dp")
    target = gather_target(sources, core, dp)
    for row, ref in enumerate(held_refs):
        some = ref.shape[0] < len(sources[0])
        given_ref[row : row + 1] = ref[pl.ds(1 + core if some else target, 1), :]
        kept_ref[row : row + 1] = ref[pl.ds(0 if some else dp, 1), :]


def pack(held, sources):
    return pl.pallas_call(
        functools.partial(pack_kernel, sources),
        out_shape=[jax.ShapeDtypeStruct((len(held), held[0].shape[1]), jnp.float32)] * 2,
        in_specs=[pl.BlockSpec(memory_space=pltpu.VMEM)] * len(held),
        out_specs=[pl.BlockSpec(memory_space=pltpu.VMEM)] * 2,
        compiler_params=pltpu.CompilerParams(vmem_limit_bytes=16 << 20),
        name="pack",
    )(*held)


def split_kernel(after_ref, *refs):
    del after_ref
    *bands, high_ref, low_ref = refs
    first = 0
    for band_ref in bands:
        for start in range(0, band_ref.shape[1], BAND):
            lanes = slice(first + start, first + start + BAND)
            high, low = split(band_ref[:, start : start + BAND])
            high_ref[:, lanes] = high.astype(jnp.bfloat16)
            low_ref[:, lanes] = low.astype(jnp.bfloat16)
        first += band_ref.shape[1]


def split_bands(bands, after):
    shape = (bands[0].shape[0], sum(band.shape[1] for band in bands))
    return pl.pallas_call(
        split_kernel,
        out_shape=[jax.ShapeDtypeStruct(shape, jnp.bfloat16)] * 2,
        in_specs=[pl.BlockSpec(memory_space=pl.ANY)]
        + [pl.BlockSpec(memory_space=pltpu.VMEM)] * len(bands),
        out_specs=[pl.BlockSpec(memory_space=pltpu.VMEM)] * 2,
        compiler_params=pltpu.CompilerParams(vmem_limit_bytes=16 << 20),
        cost_estimate=pl.CostEstimate(
            flops=0, bytes_accessed=8 * shape[0] * shape[1], transcendentals=0
        ),
        name="split",
    )(after, *bands)


def precondition_kernel(token_ref, *refs):
    del token_ref
    *refs, result_ref, held = refs
    *part_refs, high_ref, low_ref = refs
    seqs, rows = result_ref.shape[0], held.shape[1]
    core, first = lax.axis_index("tensor"), 0
    for part_ref in part_refs:
        own = jnp.where(core == 0, part_ref[:, :rows], part_ref[:, rows:])
        held[first : first + part_ref.shape[0]] = own
        first += part_ref.shape[0]
    slot = gather_slot(seqs)
    grads = jnp.concatenate(
        [held[pl.ds(slot(s), 1), :] for s in range(seqs)], axis=0
    )
    grads = jnp.concatenate(split(grads), axis=0).astype(jnp.bfloat16)
    width = high_ref.shape[1]
    for start in range(0, width, BAND):
        lanes = slice(start, start + BAND)
        by_high, by_low = (
            jnp.dot(grads, ref[:, lanes], preferred_element_type=jnp.float32)
            for ref in (high_ref, low_ref)
        )
        small = by_high[seqs:] + by_low[:seqs] + by_low[seqs:]
        result_ref[:, lanes] = by_high[:seqs] + small
    top = jnp.max(jnp.abs(result_ref[:, :width]), axis=1, keepdims=True)
    power = jnp.floor(jnp.log2(jnp.clip(top, 1e-30, 1e30))) - 14
    result_ref[:, width:] = jnp.broadcast_to(power, (seqs, BESIDE))


def precondition_rows(parts, token, matrices, seqs):
    rows, width = matrices[0].shape
    held = sum(part.shape[0] for part in parts)
    return pl.pallas_call(
        precondition_kernel,
        out_shape=jax.ShapeDtypeStruct((seqs, width + BESIDE), jnp.float32),
        in_specs=[pl.BlockSpec(memory_space=pl.ANY)]
        + [pl.BlockSpec(memory_space=pltpu.VMEM)] * (len(parts) + len(matrices)),
        out_specs=pl.BlockSpec(memory_space=pltpu.VMEM),
        scratch_shapes=[pltpu.VMEM((held, rows), jnp.float32)],
        compiler_params=pltpu.CompilerParams(vmem_limit_bytes=16 << 20),
        cost_estimate=pl.CostEstimate(
            flops=2 * seqs * rows * width,
            bytes_accessed=4 * rows * width,
            transcendentals=0,
        ),
        name="precondition",
    )(token, *parts, *matrices)


def contract_last(left, right):
    return lax.dot_general(left, right, LAST, preferred_element_type=jnp.float32)


def swap(value, axis, bit):
    size = lax.axis_size(axis)
    return lax.ppermute(value, axis, [(i, i ^ bit) for i in range(size)])


def receive(value, sources, across=0):
    pairs = [
        (2 * source + (core ^ across), 2 * chip + core)
        for core in range(2)
        for chip, source in enumerate(sources[core])
    ]
    return lax.ppermute(value, ("dp", "tensor"), pairs)


def flip(value, steps):
    size = lax.axis_size("dp")
    pairs = []
    for place in range(2 * size):
        family = (place ^ odd(place >> 1)) & 1
        pairs.append((place, place ^ (2 * steps[family] + 1)))
    return lax.ppermute(value, ("dp", "tensor"), pairs)


def odd(number):
    for shift in (8, 4, 2, 1):
        number = number ^ (number >> shift)
    return number & 1


def steps(size):
    return [1 << i for i in range(size.bit_length() - 1)]


def ordered(first, mine, other, axis):
    return jnp.where(
        first,
        jnp.concatenate((mine, other), axis),
        jnp.concatenate((other, mine), axis),
    )


def add_cores_kernel(mine_ref, other_ref, sum_ref, code_ref):
    width = sum_ref.shape[1] - BESIDE
    power = jnp.maximum(mine_ref[:, width:], other_ref[:, width:]) + 1
    scale = jnp.exp2(-power)
    for start in range(0, width, BESIDE):
        lanes = slice(start, start + BESIDE)
        total = mine_ref[:, lanes] + other_ref[:, lanes]
        sum_ref[:, lanes] = total
        code_ref[:, lanes] = total * scale
    sum_ref[:, width:] = power
    code_ref[:, width:] = power


def add_first_kernel(mine_ref, got_ref, swapped_ref, sum_ref, code_ref):
    width = sum_ref.shape[1]
    powers = [ref[:, width:] for ref in (mine_ref, got_ref, swapped_ref)]
    power = jnp.maximum(jnp.maximum(powers[0], powers[1]), powers[2]) + 2
    got_scale, swapped_scale = jnp.exp2(powers[1]), jnp.exp2(powers[2])
    scale = jnp.exp2(-power)
    own = jnp.where(lax.axis_index("tensor") == 0, 1.0, 0.0)
    for start in range(0, width, BESIDE):
        lanes = slice(start, start + BESIDE)
        first = got_ref[:, lanes] * got_scale + swapped_ref[:, lanes] * swapped_scale
        mine = mine_ref[:, lanes]
        sum_ref[:, lanes] = mine + first
        code_ref[:, lanes] = (first + mine * own) * scale
    code_ref[:, width:] = power


def score_kernel(sum_ref, got_ref, swapped_ref, query_ref, result_ref, whole):
    width = sum_ref.shape[1]
    got_scale = jnp.exp2(got_ref[:, width:])
    swapped_scale = jnp.exp2(swapped_ref[:, width:])
    for start in range(0, width, BESIDE):
        lanes = slice(start, start + BESIDE)
        second = got_ref[:, lanes] * got_scale + swapped_ref[:, lanes] * swapped_scale
        whole[:, lanes] = sum_ref[:, lanes] + second
    scores = contract_last(whole[...].astype(query_ref.dtype), query_ref[...])
    result_ref[...] = scores * (1 / math.sqrt(width))


def small_kernel(kernel, name, operands, shapes, scratch=()):
    return pl.pallas_call(
        kernel,
        out_shape=[jax.ShapeDtypeStruct(shape, jnp.float32) for shape in shapes],
        in_specs=[pl.BlockSpec(memory_space=pltpu.VMEM)] * len(operands),
        out_specs=[pl.BlockSpec(memory_space=pltpu.VMEM)] * len(shapes),
        scratch_shapes=scratch,
        compiler_params=pltpu.CompilerParams(vmem_limit_bytes=16 << 20),
        name=name,
    )(*operands)


def score_by_rounds(partial, query_grads):
    def heard(code, sources, across):
        got = receive(code.astype(jnp.float16), sources, across)
        swapped = swap(got, "tensor", 1)
        return got.astype(jnp.float32), swapped.astype(jnp.float32)

    seqs, extent = partial.shape
    wide, narrow = (seqs, extent), (seqs, extent - BESIDE)
    other = swap(partial, "tensor", 1)
    mine, code = small_kernel(
        add_cores_kernel, "add_cores", (partial, other), (wide, wide)
    )
    heard_first = heard(code, ROUNDS_OF_8[0], 0)
    total, code = small_kernel(
        add_first_kernel, "add_first", (mine, *heard_first), (narrow, wide)
    )
    heard_second = heard(code, ROUNDS_OF_8[1], 0)
    return small_kernel(
        score_kernel,
        "score",
        (total, *heard_second, query_grads),
        ((seqs, query_grads.shape[0]),),
        [pltpu.VMEM(narrow, jnp.float32)],
    )[0]


def add_steps(partial):
    half = (partial.shape[1] - BESIDE) // 2
    even = lax.axis_index("tensor") == odd(lax.axis_index("dp"))
    low, high = partial[:, :half], partial[:, half : 2 * half]
    given = jnp.where(even, high, low)
    total = jnp.where(even, low, high) + swap(given, "tensor", 1)
    bits = steps(lax.axis_size("dp"))
    for pair in zip(bits, bits[::-1]):
        total = total + flip(total, pair)
    return ordered(even, total, swap(total, "tensor", 1), 1)


def on_device(layer_input, gate_grad, factor_in, factor_out, precondition, query_grads):
    own_rows, width = precondition.shape
    dp, dp_size = lax.axis_index("dp"), lax.axis_size("dp")

    sides = project(layer_input, gate_grad, factor_in, factor_out)
    other = swap(sides, "tensor", 1)
    gradient, *firsts = gradient_rows(sides, other, dp_size)

    held = [gradient]
    rounds = gather_rounds(dp_size)
    for number, (sources, swaps) in enumerate(rounds):
        if number == len(rounds) - 1:
            given, kept = pack(held, sources)
            got = receive(given, sources)
            parts = [kept, got] + ([swap(got, "tensor", 1)] if swaps else [])
        else:
            given = (*firsts, *held)[0] if number == 0 else jnp.stack(held)
            got = receive(given, sources)
            heard = [got] + ([swap(got, "tensor", 1)] if swaps else [])
            held += [row for rows in heard for row in (rows if number else [rows])]
    rows, _ = lax.optimization_barrier((precondition, sides))
    matrices = split_bands([rows], got)

    partial = precondition_rows(parts, got, matrices, dp_size)

    if dp_size == 8:
        return score_by_rounds(partial, query_grads)
    rounded = add_steps(partial).astype(jnp.bfloat16)
    return contract_last(rounded, query_grads) * (1 / math.sqrt(width))


def solution(mesh):
    in_specs = (
        P(("groups", "dp"), "tensor"),
        P(("groups", "dp"), "tensor"),
        P(None, "tensor"),
        P(None, "tensor"),
        P(("dp", "tensor"), None),
        P(("dp", "tensor"), None),
    )
    out_specs = P("groups", ("dp", "tensor"))
    return jax.shard_map(
        on_device, mesh=mesh, in_specs=in_specs, out_specs=out_specs, check_vma=False
    )
```
